256 devices in a mesh: head: 8 (over x, y_hi), ctx: 32 (over z, y_lo, core).
Axes of the slice: x: 4, y: 4 (y_hi: 2, y_lo: 2; y = y_hi * 2 + y_lo), z: 8, core: 2. Of those that a mesh axis runs over, the one named last changes fastest.
Arguments:
- queries: bfloat16 [8192, 1024], P('ctx', 'head'), may hold values from -6 to 6
- keys: bfloat16 [8192, 1024], P('ctx', 'head'), may hold values from -6 to 6
- values: bfloat16 [8192, 1024], P('ctx', 'head'), may hold values from -6 to 6
- teacher_rows: bfloat16 [12288, 1024], P(('head', 'ctx')), may hold values from -3 to 3
- slots: int32 [12288], P(('head', 'ctx')), may hold values from 0 to 95, as said below
- spans: int32 [12288, 2], P(('head', 'ctx')), may hold values from 0 to 256, as said below
Outputs:
- grad_queries: bfloat16 [8192, 1024], P('ctx', 'head')
- grad_keys: bfloat16 [8192, 1024], P('ctx', 'head')
- grad_values: bfloat16 [8192, 1024], P('ctx', 'head')
The draws below stay inside these ranges and needn't reach their ends.
Inputs may be any that keep to these rules, and one draw needn't show every extreme that they name: `slots`: in each block of 48 rows (the rows of one device) the values are distinct, so no block has more than 3 rows whose value // 3 is the same; in every draw one index of ctx gets exactly 3 rows from every block. `spans`: each span lies within the 256 student tokens of its index of ctx and covers 1 to 8 of them; some span covers exactly 8 and some ends at 256.
All inputs are finite; a program needn't handle non-finite values.
Results may differ from the reference program's by a relative error of at most 0.0076.
Values may be sent and summed in bfloat16 or wider, within the bound.
A program may use at most 64 MiB of HBM per device.

```python
import math
import jax
import jax.numpy as jnp
from jax import lax

H = 8
DH = 128
S_DEV = 256
SPAN = 8
TOKENS = 8192
TROWS = 12288
TR_DEV = 48
CAP = 3
N_HEAD = 8
N_CTX = 32


def draw_queries(key, part):
    key = jax.random.fold_in(key, 1)
    full_shape = (TOKENS, H * DH)
    result = jax.random.truncated_normal(key, -6.0, 6.0, full_shape, jnp.float32)
    return result.astype(jnp.bfloat16)


def draw_keys(key, part):
    key = jax.random.fold_in(key, 2)
    full_shape = (TOKENS, H * DH)
    result = jax.random.truncated_normal(key, -6.0, 6.0, full_shape, jnp.float32)
    return result.astype(jnp.bfloat16)


def draw_slots(key, part):
    key = jax.random.fold_in(key, 3)
    first, second = jax.random.split(key)
    slot_count = N_CTX * CAP
    full_target = jax.random.randint(first, (), 0, N_CTX)

    def one_block(block_key):
        order = jax.random.permutation(block_key, slot_count)
        priority = jnp.where(order // CAP == full_target, -1, jnp.arange(slot_count, dtype=jnp.int32))
        picked = jnp.argsort(priority, stable=True)
        return order[picked[:TR_DEV]]
    block_keys = jax.random.split(second, N_HEAD * N_CTX)
    return jax.vmap(one_block)(block_keys).reshape(-1).astype(jnp.int32)


def draw_spans(key, part):
    key = jax.random.fold_in(key, 4)
    first, second = jax.random.split(key)
    row_ids = jnp.arange(TROWS, dtype=jnp.int32)
    lengths = jax.random.randint(first, (TROWS,), 1, SPAN + 1)
    lengths = jnp.where(row_ids % TR_DEV == 1, SPAN, lengths)
    starts = jax.random.randint(second, (TROWS,), 0, 1048576) % (S_DEV - lengths + 1)
    starts = jnp.where(row_ids % TR_DEV == 0, S_DEV - lengths, starts)
    return jnp.stack([starts, starts + lengths], axis=1).astype(jnp.int32)


def shard_levels(key, shape, pieces, smallest, top_value):
    loudness = 1.0
    for position, blocks in pieces:
        heights = jax.random.uniform(jax.random.fold_in(jax.random.fold_in(key, 6), position), (blocks,), jnp.float32, smallest / len(pieces), top_value / len(pieces))
        loudness = loudness * jnp.repeat(jnp.exp(heights), shape[position] // blocks).reshape((-1,) + (1,) * (len(shape) - 1 - position))
    return loudness


def centred(key, dims, deviation, reach, cuts=(), kind=jnp.bfloat16):
    values = jax.random.normal(key, dims, jnp.float32) * deviation
    if len(cuts) > 0:
        values = shard_levels(key, dims, cuts, -0.22, 0.18) * values
    return jnp.clip(values, min=-reach, max=reach).astype(kind)


def setup_inputs(seed: int = 0) -> dict:
    key_of = jax.random.split(jax.random.key(seed), 7)
    queries = draw_queries(jax.random.fold_in(key_of[6], 71), 0)
    keys = draw_keys(jax.random.fold_in(key_of[6], 71), 0)
    values = centred(key_of[2], (TOKENS, H * DH), 1.0, 6.0, ((0, 32), (1, 8)))
    teacher_rows = centred(key_of[3], (TROWS, H * DH), 0.5, 3.0, ((0, 256),))
    slots = draw_slots(jax.random.fold_in(key_of[6], 71), 0)
    spans = draw_spans(jax.random.fold_in(key_of[6], 71), 0)
    return {"queries": queries, "keys": keys, "values": values, "teacher_rows": teacher_rows, "slots": slots, "spans": spans}


masked_value = -1e+30

def reference(queries, keys, values, teacher_rows, slots, spans):
    score_scale = 1.0 / math.sqrt(DH)
    target = (slots // CAP).astype(jnp.int32) * S_DEV
    lower = target + spans[:, 0]
    upper = target + spans[:, 1]

    def grad_block(block_index):
        token_pos = block_index * S_DEV + jnp.arange(S_DEV, dtype=jnp.int32)
        coverage = ((token_pos[:, None] >= lower[None, :]) & (token_pos[:, None] < upper[None, :])).astype(jnp.bfloat16)
        return jnp.dot(coverage, teacher_rows, preferred_element_type=jnp.float32).astype(jnp.bfloat16)
    grad_rows = lax.map(grad_block, jnp.arange(N_CTX, dtype=jnp.int32)).reshape(TOKENS, H * DH)

    def split_heads(array):
        return array.reshape(TOKENS, H, DH).transpose(1, 0, 2)

    def merge_heads(array):
        return array.transpose(1, 0, 2).reshape(TOKENS, H * DH)

    def head_grads(operands):
        query_head, key_head, value_head, grad_head = operands
        token_ids = jnp.arange(TOKENS, dtype=jnp.int32)

        def step_fn(running, block_index):
            key_acc, value_acc = running
            row_start = block_index * S_DEV
            query_rows = lax.dynamic_slice_in_dim(query_head, row_start, S_DEV, 0)
            grad_block_rows = lax.dynamic_slice_in_dim(grad_head, row_start, S_DEV, 0)
            row_ids = row_start + jnp.arange(S_DEV, dtype=jnp.int32)
            visible = token_ids[None, :] <= row_ids[:, None]
            scores = jnp.dot(query_rows, key_head.T, preferred_element_type=jnp.float32) * score_scale
            scores = jnp.where(visible, scores, masked_value)
            row_top = lax.optimization_barrier(jnp.max(scores, axis=1, keepdims=True))
            row_total = lax.optimization_barrier(jnp.sum(jnp.exp(scores - row_top), axis=1, keepdims=True))
            row_lse = row_top + jnp.log(row_total)
            prob = jnp.where(visible, jnp.exp(scores - row_lse), 0.0)
            grad_prob = jnp.dot(grad_block_rows, value_head.T, preferred_element_type=jnp.float32)
            row_delta = lax.optimization_barrier(jnp.sum(prob * grad_prob, axis=1, keepdims=True))
            dscore = (prob * (grad_prob - row_delta) * score_scale).astype(jnp.bfloat16)
            prob_half = prob.astype(jnp.bfloat16)
            value_acc = value_acc + jnp.dot(prob_half.T, grad_block_rows, preferred_element_type=jnp.float32)
            key_acc = key_acc + jnp.dot(dscore.T, query_rows, preferred_element_type=jnp.float32)
            query_part = jnp.dot(dscore, key_head, preferred_element_type=jnp.float32).astype(jnp.bfloat16)
            return ((key_acc, value_acc), query_part)
        zero_sums = jnp.zeros((TOKENS, DH), jnp.float32)
        sums, query_parts = lax.scan(step_fn, (zero_sums, zero_sums), jnp.arange(N_CTX, dtype=jnp.int32))
        return (query_parts.reshape(TOKENS, DH), sums[0].astype(jnp.bfloat16), sums[1].astype(jnp.bfloat16))
    grad_q, grad_k, grad_v = lax.map(head_grads, (split_heads(queries), split_heads(keys), split_heads(values), split_heads(grad_rows)))
    return (merge_heads(grad_q), merge_heads(grad_k), merge_heads(grad_v))
```

```python
import functools
import math

import jax
import jax.numpy as jnp
from jax import lax
from jax.experimental import pallas as pl
from jax.experimental.pallas import tpu as pltpu
from jax.sharding import PartitionSpec as P

DH = 128
CAP = 3
GROUP = 8
CHUNK = 512
MASKED = -1e30
MESH = pl.DeviceIdType.MESH
F32 = jnp.float32
BF16 = jnp.bfloat16


def dot_nt(a, b):
    return lax.dot_general(a, b, (((1,), (1,)), ((), ())), preferred_element_type=F32)


def dot_nn(a, b):
    return lax.dot_general(a, b, (((1,), (0,)), ((), ())), preferred_element_type=F32)


def iota(shape, dim):
    return lax.broadcasted_iota(jnp.int32, shape, dim)


def kernel(
    heads,
    ctxs,
    group,
    q_ref,
    k_ref,
    v_ref,
    t_ref,
    slots_ref,
    spans_ref,
    dq_ref,
    dk_ref,
    dv_ref,
    hop1_out,
    hop1_in,
    hop2_out,
    hop2_in,
    qg,
    dog,
    kv,
    kt,
    pt,
    dp,
    mrow,
    lrow,
    st,
    frow,
    drow,
    dqa,
    dq_out,
    dq_in,
    dkv_out,
    dkv_in,
    dkv_own,
    h_send,
    h_recv,
    c_send,
    c_recv,
    q_send,
    q_recv,
    kv_send,
    kv_recv,
    do_send,
    do_recv,
    st_send,
    st_recv,
    dq_send,
    dq_recv,
    dkv_send,
    dkv_recv,
):
    me_h = lax.axis_index("head")
    me_c = lax.axis_index("ctx")
    z = lax.div(me_c, group)
    r = lax.rem(me_c, group)
    base = z * group
    rows = q_ref.shape[0]
    trows = t_ref.shape[0]
    lines = ctxs // group
    chunks = group * rows // CHUNK
    per_chunk = CHUNK // rows
    scale = 1.0 / math.sqrt(DH)

    def group_peer(i):
        return lax.rem(r + i, group)

    def remote(src, dst, send, recv, device):
        return pltpu.make_async_remote_copy(
            src_ref=src,
            dst_ref=dst,
            send_sem=send,
            recv_sem=recv,
            device_id=device,
            device_id_type=MESH,
        )

    barrier = pltpu.get_barrier_semaphore()

    def greet_head(i, carry):
        pl.semaphore_signal(
            barrier, inc=1, device_id=(lax.rem(me_h + i, heads), me_c), device_id_type=MESH
        )
        return carry

    def greet_ctx(i, carry):
        pl.semaphore_signal(
            barrier, inc=1, device_id=(me_h, lax.rem(me_c + i, ctxs)), device_id_type=MESH
        )
        return carry

    lax.fori_loop(1, heads, greet_head, 0)
    lax.fori_loop(1, ctxs, greet_ctx, 0)

    lane = iota((trows, DH), 1)
    spans = spans_ref[...]
    meta = jnp.where(lane < 64, spans[:, 0:1], spans[:, 1:2]).astype(F32).astype(BF16)
    pick = (jnp.bitwise_and(iota((trows, DH), 1), 63) == iota((trows, DH), 0)).astype(BF16)
    slot_in = jnp.broadcast_to(slots_ref[...].astype(F32), (16, trows)).astype(BF16)
    slot_lanes = dot_nn(slot_in, pick)
    slot_lanes = jnp.where(
        jnp.bitwise_and(iota((16, DH), 1), 63) < trows, slot_lanes, -1.0
    ).astype(BF16)
    for h in range(heads):
        hop1_out[h, 0:trows, :] = t_ref[:, h * DH : (h + 1) * DH]
        hop1_out[h, trows:64, :] = jnp.zeros((64 - trows, DH), BF16)
        hop1_out[h, 64 : 64 + trows, :] = meta
        if trows < 48:
            hop1_out[h, 64 + trows : 112, :] = jnp.zeros((48 - trows, DH), BF16)
        hop1_out[h, 112:128, :] = slot_lanes
    own_q = pl.ds(pl.multiple_of(r * rows, rows), rows)
    qg[own_q, :] = q_ref[...]
    kv[z, 0] = k_ref[...]
    kv[z, 1] = v_ref[...]

    pl.semaphore_wait(barrier, heads - 1 + ctxs - 1)

    def hop1(i):
        peer = lax.rem(me_h + i, heads)
        return peer, remote(
            hop1_out.at[peer], hop1_in.at[me_h], h_send.at[i], h_recv.at[me_h], (peer, me_c)
        )

    def hop1_start(i, carry):
        hop1(i)[1].start()
        return carry

    lax.fori_loop(1, heads, hop1_start, 0)
    hop1_in[me_h] = hop1_out[me_h]

    def q_copy(i):
        return remote(
            qg.at[own_q, :],
            qg.at[own_q, :],
            q_send.at[i],
            q_recv.at[r],
            (me_h, base + group_peer(i)),
        )

    def q_start(i, carry):
        q_copy(i).start()
        return carry

    lax.fori_loop(1, group, q_start, 0)

    def kv_copy(later):
        return remote(
            kv.at[z], kv.at[z], kv_send.at[later], kv_recv.at[z], (me_h, later * group + r)
        )

    def kv_start(later, carry):
        kv_copy(later).start()
        return carry

    lax.fori_loop(z + 1, lines, kv_start, 0)

    def hop1_wait(i, carry):
        peer = lax.rem(me_h + i, heads)
        remote(
            hop1_out.at[peer], hop1_in.at[peer], h_send.at[i], h_recv.at[peer], (peer, me_c)
        ).wait_recv()
        return carry

    lax.fori_loop(1, heads, hop1_wait, 0)

    kdepth = heads * 64
    teacher = hop1_in[:, 0:64, :].reshape(kdepth, DH)
    bounds = hop1_in[:, 64:128, :].reshape(kdepth, DH).astype(F32)
    swapped = pltpu.roll(bounds, 64, 1)
    left = iota((kdepth, DH), 1) < 64
    first = jnp.where(left, bounds, swapped).astype(BF16)
    last = jnp.where(left, swapped, bounds).astype(BF16)
    codes = []
    lane1 = iota((1, DH), 1)
    for pair in range(heads // 2):
        even = hop1_in[2 * pair, 112:128, :].astype(F32)[0:1]
        odd = hop1_in[2 * pair + 1, 112:128, :].astype(F32)[0:1]
        even = jnp.where(even < 0.0, -1.0, even + 128.0 * (2 * pair))
        odd = jnp.where(odd < 0.0, -1.0, odd + 128.0 * (2 * pair + 1))
        codes.append(jnp.where(lane1 < 64, even, odd))
    mine = lax.rem(me_c, 4) * 32

    def pack(step, carry):
        row = iota((256, DH), 0)
        within = jnp.bitwise_and(row, 31)
        dest = lax.shift_right_logical(row, 5) + step * 8
        place = lax.div(within, heads)
        head = within - place * heads
        wanted = jnp.where(place < CAP, dest * CAP + place + 128 * head, -5).astype(F32)
        chosen = [(wanted == code).astype(F32).astype(BF16) for code in codes]
        chosen = jnp.concatenate(chosen, axis=1)
        moved = dot_nn(chosen, teacher).reshape(8, 32, DH)
        diagonal = (iota((256, DH), 1) == within + mine).astype(F32)
        lower = (dot_nn(chosen, first) * diagonal).reshape(8, 32, DH)
        upper = (dot_nn(chosen, last) * diagonal).reshape(8, 32, DH)
        lower = jnp.sum(lower, axis=1, keepdims=True)
        upper = jnp.sum(upper, axis=1, keepdims=True)
        line = iota((8, 8, DH), 1)
        tail = jnp.where(line == 0, lower, jnp.where(line == 1, upper, 0.0))
        message = jnp.concatenate([moved[:, 0:24, :], tail], axis=1)
        hop2_out[pl.ds(step * 8, 8)] = message.astype(BF16)
        return carry

    lax.fori_loop(0, ctxs // 8, pack, 0)

    def hop2_start(i, carry):
        peer = lax.rem(me_c + i, ctxs)
        remote(
            hop2_out.at[peer], hop2_in.at[me_c], c_send.at[i], c_recv.at[me_c], (me_h, peer)
        ).start()
        return carry

    lax.fori_loop(1, ctxs, hop2_start, 0)
    hop2_in[me_c] = hop2_out[me_c]

    def q_wait(i, carry):
        src = pl.ds(pl.multiple_of(group_peer(i) * rows, rows), rows)
        remote(
            qg.at[src, :],
            qg.at[src, :],
            q_send.at[i],
            q_recv.at[group_peer(i)],
            (me_h, base + group_peer(i)),
        ).wait_recv()
        return carry

    lax.fori_loop(1, group, q_wait, 0)

    def kv_wait(earlier, carry):
        remote(
            kv.at[earlier],
            kv.at[earlier],
            kv_send.at[earlier],
            kv_recv.at[earlier],
            (me_h, earlier * group + r),
        ).wait_recv()
        return carry

    lax.fori_loop(0, z, kv_wait, 0)

    def transpose_keys(line, carry):
        kt[line] = kv[line, 0].astype(F32).T.astype(BF16)
        return carry

    lax.fori_loop(0, z + 1, transpose_keys, 0)

    def scores_chunk(qc, carry):
        queries = qg[pl.ds(pl.multiple_of(qc * CHUNK, CHUNK), CHUNK), :]

        def score(line, top):
            s = dot_nt(kv[line, 0], queries)
            pt[line, qc] = s
            return jnp.maximum(top, jnp.max(s, axis=0, keepdims=True))

        top = lax.fori_loop(0, z, score, jnp.full((1, CHUNK), MASKED, F32))
        s = dot_nt(kv[z, 0], queries)
        key_pos = iota((rows, CHUNK), 0) + r * rows
        query_pos = iota((rows, CHUNK), 1) + qc * CHUNK
        s = jnp.where(key_pos <= query_pos, s, MASKED)
        pt[z, qc] = s
        top = jnp.maximum(top, jnp.max(s, axis=0, keepdims=True))

        def weight(line, total):
            p = jnp.exp((pt[line, qc] - top) * scale)
            pt[line, qc] = p
            return total + jnp.sum(p, axis=0, keepdims=True)

        total = lax.fori_loop(0, z + 1, weight, jnp.zeros((1, CHUNK), F32))
        mrow[qc] = top * scale
        lrow[qc] = total
        return carry

    lax.fori_loop(0, chunks, scores_chunk, 0)

    def hop2_wait(i, carry):
        peer = lax.rem(me_c + i, ctxs)
        remote(
            hop2_out.at[peer], hop2_in.at[peer], c_send.at[i], c_recv.at[peer], (me_h, peer)
        ).wait_recv()
        return carry

    lax.fori_loop(1, ctxs, hop2_wait, 0)
    token = iota((rows, DH), 0).astype(F32)

    def cover(step, total):
        four = hop2_in[pl.ds(step * 4, 4)]
        edges = jnp.sum(four[:, 16:32, :].astype(F32), axis=0)
        lower = edges[8:9]
        upper = edges[9:10]
        covered = jnp.where((token >= lower) & (token < upper), 1.0, 0.0).astype(BF16)
        return total + dot_nn(covered, four.reshape(4 * 32, DH))

    grad = lax.fori_loop(0, ctxs // 4, cover, jnp.zeros((rows, DH), F32))
    dog[own_q, :] = grad.astype(BF16)

    def do_start(i, carry):
        remote(
            dog.at[own_q, :],
            dog.at[own_q, :],
            do_send.at[i],
            do_recv.at[r],
            (me_h, base + group_peer(i)),
        ).start()
        return carry

    lax.fori_loop(1, group, do_start, 0)

    def do_wait(i, carry):
        src = pl.ds(pl.multiple_of(group_peer(i) * rows, rows), rows)
        remote(
            dog.at[src, :],
            dog.at[src, :],
            do_send.at[i],
            do_recv.at[group_peer(i)],
            (me_h, base + group_peer(i)),
        ).wait_recv()
        return carry

    lax.fori_loop(1, group, do_wait, 0)

    for qc in range(chunks):
        grads = dog[qc * CHUNK : (qc + 1) * CHUNK, :]

        def grad_prob(line, weighted, qc=qc, grads=grads):
            d = dot_nt(kv[line, 1], grads)
            dp[line, qc] = d
            return weighted + jnp.sum(pt[line, qc] * d, axis=0, keepdims=True)

        weighted = lax.fori_loop(0, z + 1, grad_prob, jnp.zeros((1, CHUNK), F32))
        total = lrow[qc]
        st[r, 2 * qc : 2 * qc + 1, :] = mrow[qc] + jnp.log(total)
        st[r, 2 * qc + 1 : 2 * qc + 2, :] = weighted / total

    def st_copy(i):
        return remote(
            st.at[r], st.at[r], st_send.at[i], st_recv.at[r], (me_h, base + group_peer(i))
        )

    def st_start(i, carry):
        st_copy(i).start()
        return carry

    lax.fori_loop(1, group, st_start, 0)

    def st_wait(i, carry):
        src = group_peer(i)
        remote(
            st.at[src], st.at[src], st_send.at[i], st_recv.at[src], (me_h, base + src)
        ).wait_recv()
        return carry

    lax.fori_loop(1, group, st_wait, 0)

    for qc in range(chunks):
        parts = st[:, 2 * qc : 2 * qc + 1, :]
        deltas = st[:, 2 * qc + 1 : 2 * qc + 2, :]
        top = jnp.max(parts, axis=0)
        lse = top + jnp.log(jnp.sum(jnp.exp(parts - top[None]), axis=0))
        drow[qc] = jnp.sum(jnp.exp(parts - lse[None]) * deltas, axis=0)
        frow[qc] = jnp.exp(mrow[qc] - lse)

    for qc in range(group):
        dqa[qc] = jnp.zeros((DH, rows), F32)

    def key_terms(line):
        key_sum = jnp.zeros((rows, DH), F32)
        value_sum = jnp.zeros((rows, DH), F32)
        for qc in range(chunks):
            here = slice(qc * CHUNK, (qc + 1) * CHUNK)
            prob = pt[line, qc] * frow[qc]
            dscore = (prob * (dp[line, qc] - drow[qc]) * scale).astype(BF16)
            value_sum += dot_nn(prob.astype(BF16), dog[here, :])
            key_sum += dot_nn(dscore, qg[here, :])
            part = dot_nn(kt[line], dscore)
            for j in range(per_chunk):
                dqa[qc * per_chunk + j] += part[:, j * rows : (j + 1) * rows]
        return key_sum, value_sum

    def dkv_copy(line):
        return remote(
            dkv_out.at[line],
            dkv_in.at[z],
            dkv_send.at[line],
            dkv_recv.at[z],
            (me_h, line * group + r),
        )

    def earlier_keys(line, carry):
        key_sum, value_sum = key_terms(line)
        dkv_out[line, 0] = key_sum.astype(BF16)
        dkv_out[line, 1] = value_sum.astype(BF16)
        dkv_copy(line).start()
        return carry

    lax.fori_loop(0, z, earlier_keys, 0)
    key_sum, value_sum = key_terms(z)
    dkv_own[0] = key_sum
    dkv_own[1] = value_sum

    dq_out[...] = dqa[...].astype(BF16)

    def dq_copy(i):
        peer = group_peer(i)
        return remote(
            dq_out.at[peer], dq_in.at[r], dq_send.at[i], dq_recv.at[r], (me_h, base + peer)
        )

    def dq_start(i, carry):
        dq_copy(i).start()
        return carry

    lax.fori_loop(1, group, dq_start, 0)

    def dkv_add(later, carry):
        remote(
            dkv_out.at[later],
            dkv_in.at[later],
            dkv_send.at[later],
            dkv_recv.at[later],
            (me_h, later * group + r),
        ).wait_recv()
        dkv_own[...] += dkv_in[later].astype(F32)
        return carry

    lax.fori_loop(z + 1, lines, dkv_add, 0)
    dk_ref[...] = dkv_own[0].astype(BF16)
    dv_ref[...] = dkv_own[1].astype(BF16)

    def dq_add(i, total):
        src = group_peer(i)
        remote(
            dq_out.at[src], dq_in.at[src], dq_send.at[i], dq_recv.at[src], (me_h, base + src)
        ).wait_recv()
        return total + dq_in[src].astype(F32)

    total = lax.fori_loop(1, group, dq_add, dqa[r])
    dq_ref[...] = total.T.astype(BF16)

    def hop1_sent(i, carry):
        hop1(i)[1].wait_send()
        return carry

    lax.fori_loop(1, heads, hop1_sent, 0)

    def hop2_sent(i, carry):
        peer = lax.rem(me_c + i, ctxs)
        remote(
            hop2_out.at[peer], hop2_in.at[me_c], c_send.at[i], c_recv.at[me_c], (me_h, peer)
        ).wait_send()
        return carry

    lax.fori_loop(1, ctxs, hop2_sent, 0)

    def group_sent(i, carry):
        q_copy(i).wait_send()
        remote(
            dog.at[own_q, :],
            dog.at[own_q, :],
            do_send.at[i],
            do_recv.at[r],
            (me_h, base + group_peer(i)),
        ).wait_send()
        st_copy(i).wait_send()
        dq_copy(i).wait_send()
        return carry

    lax.fori_loop(1, group, group_sent, 0)

    def kv_sent(later, carry):
        kv_copy(later).wait_send()
        return carry

    lax.fori_loop(z + 1, lines, kv_sent, 0)

    def dkv_sent(line, carry):
        dkv_copy(line).wait_send()
        return carry

    lax.fori_loop(0, z, dkv_sent, 0)


def shards(heads, ctxs, group, queries, keys, values, teacher_rows, slots, spans):
    rows = queries.shape[0]
    trows = teacher_rows.shape[0]
    lines = ctxs // group
    chunks = group * rows // CHUNK
    vm = pltpu.VMEM
    dma = pltpu.SemaphoreType.DMA
    scratch = [
        vm((heads, 128, DH), BF16),
        vm((heads, 128, DH), BF16),
        vm((ctxs, 32, DH), BF16),
        vm((ctxs, 32, DH), BF16),
        vm((group * rows, DH), BF16),
        vm((group * rows, DH), BF16),
        vm((lines, 2, rows, DH), BF16),
        vm((lines, DH, rows), BF16),
        vm((lines, chunks, rows, CHUNK), F32),
        vm((lines, chunks, rows, CHUNK), F32),
        vm((chunks, 1, CHUNK), F32),
        vm((chunks, 1, CHUNK), F32),
        vm((group, 2 * chunks, CHUNK), F32),
        vm((chunks, 1, CHUNK), F32),
        vm((chunks, 1, CHUNK), F32),
        vm((group, DH, rows), F32),
        vm((group, DH, rows), BF16),
        vm((group, DH, rows), BF16),
        vm((lines, 2, rows, DH), BF16),
        vm((lines, 2, rows, DH), BF16),
        vm((2, rows, DH), F32),
        dma((heads,)),
        dma((heads,)),
        dma((ctxs,)),
        dma((ctxs,)),
        dma((group,)),
        dma((group,)),
        dma((lines,)),
        dma((lines,)),
        dma((group,)),
        dma((group,)),
        dma((group,)),
        dma((group,)),
        dma((group,)),
        dma((group,)),
        dma((lines,)),
        dma((lines,)),
    ]
    out = jax.ShapeDtypeStruct((rows, DH), BF16)
    return pl.pallas_call(
        functools.partial(kernel, heads, ctxs, group),
        out_shape=(out, out, out),
        in_specs=[pl.BlockSpec(memory_space=pltpu.VMEM)] * 6,
        out_specs=(pl.BlockSpec(memory_space=pltpu.VMEM),) * 3,
        scratch_shapes=scratch,
        compiler_params=pltpu.CompilerParams(
            collective_id=0, has_side_effects=True, vmem_limit_bytes=48 * 1024 * 1024
        ),
        name="attention_backward",
    )(queries, keys, values, teacher_rows, slots.reshape(1, trows), spans)


def solution(mesh):
    heads, ctxs = mesh.shape["head"], mesh.shape["ctx"]
    group = min(GROUP, ctxs // 2)
    return jax.shard_map(
        functools.partial(shards, heads, ctxs, group),
        mesh=mesh,
        in_specs=(
            P("ctx", "head"),
            P("ctx", "head"),
            P("ctx", "head"),
            P(("head", "ctx"), None),
            P(("head", "ctx")),
            P(("head", "ctx"), None),
        ),
        out_specs=(P("ctx", "head"), P("ctx", "head"), P("ctx", "head")),
        check_vma=False,
    )
```

```python
import functools
import math

import jax
import jax.numpy as jnp
from jax import lax
from jax.experimental import pallas as pl
from jax.experimental.pallas import tpu as pltpu
from jax.sharding import PartitionSpec as P

DH = 128
CAP = 3
GROUP = 8
CHUNK = 512
MASKED = -1e30
MESH = pl.DeviceIdType.MESH
F32 = jnp.float32
BF16 = jnp.bfloat16


def dot_nt(a, b):
    return lax.dot_general(a, b, (((1,), (1,)), ((), ())), preferred_element_type=F32)


def dot_nn(a, b):
    return lax.dot_general(a, b, (((1,), (0,)), ((), ())), preferred_element_type=F32)


def iota(shape, dim):
    return lax.broadcasted_iota(jnp.int32, shape, dim)


def kernel(heads, ctxs, group, *refs):
    (q_hbm, k_hbm, v_hbm, t_hbm, slots_hbm, spans_hbm, dq_ref, dk_ref, dv_ref) = refs[:9]
    (slots_in, spans_in, hop1_out, hop1_in, hop2_out, hop2_in) = refs[9:15]
    (qg, dog, kb, vb, kt, pt, p16, dp, mrow, lse_st, del_st, drow) = refs[15:27]
    (dqa, dq_out, dq_sib, dq_far, dq_in) = refs[27:32]
    (dk_out, dk_in, dk_own, dv_out, dv_in, dv_own) = refs[32:38]
    (in_sem, h_send, h_recv, c_send, c_recv, q_send, q_recv, k_send, k_recv) = refs[38:47]
    (v_send, v_recv, do_send, do_recv, l_send, l_recv, d_send, d_recv) = refs[47:55]
    (s_send, s_recv, dq_send, dq_recv, dk_send, dk_recv, dv_send, dv_recv) = refs[55:63]
    me_h = lax.axis_index("head")
    me_c = lax.axis_index("ctx")
    z = lax.div(me_c, group)
    r = lax.rem(me_c, group)
    base = z * group
    core = lax.rem(r, 2)
    chip = lax.div(r, 2)
    chips = group // 2
    sibling = r + 1 - 2 * core
    rows = dq_ref.shape[0]
    trows = t_hbm.shape[0]
    lines = ctxs // group
    chunks = group * rows // CHUNK
    per_chunk = CHUNK // rows
    scale = 1.0 / math.sqrt(DH)

    def each(start, stop, f):
        def body(i, carry):
            f(i)
            return carry

        lax.fori_loop(start, stop, body, 0)

    def group_peer(i):
        return lax.rem(r + i, group)

    def far_peer(i):
        return lax.rem(r + 2 * i, group)

    def block(index):
        return pl.ds(pl.multiple_of(index * rows, rows), rows)

    def remote(src, dst, send, recv, device):
        return pltpu.make_async_remote_copy(
            src_ref=src,
            dst_ref=dst,
            send_sem=send,
            recv_sem=recv,
            device_id=device,
            device_id_type=MESH,
        )

    def hop1(i):
        peer = lax.rem(me_h + i, heads)
        return remote(
            hop1_out.at[peer], hop1_in.at[me_h], h_send.at[i], h_recv.at[me_h], (peer, me_c)
        )

    def hop1_arrival(i):
        peer = lax.rem(me_h + i, heads)
        return remote(
            hop1_out.at[peer], hop1_in.at[peer], h_send.at[i], h_recv.at[peer], (peer, me_c)
        )

    def hop2(i):
        peer = lax.rem(me_c + i, ctxs)
        return remote(
            hop2_out.at[peer], hop2_in.at[me_c], c_send.at[i], c_recv.at[me_c], (me_h, peer)
        )

    def hop2_arrival(i):
        peer = lax.rem(me_c + i, ctxs)
        return remote(
            hop2_out.at[peer], hop2_in.at[peer], c_send.at[i], c_recv.at[peer], (me_h, peer)
        )

    def share(buffer, send, recv, which, index, peer):
        here = buffer.at[block(which), :]
        return remote(here, here, send.at[index], recv.at[which], (me_h, base + peer))

    def share_far(buffer, send, recv, i):
        return share(buffer, send, recv, r, i, far_peer(i))

    def share_near(buffer, send, recv):
        return share(buffer, send, recv, r, 0, sibling)

    def share_on(buffer, send, recv, i):
        return share(buffer, send, recv, far_peer(i), chips + i, sibling)

    def share_start(buffer, send, recv):
        each(1, chips, lambda i: share_far(buffer, send, recv, i).start())
        share_near(buffer, send, recv).start()

    def share_forward(buffer, send, recv):
        def step(i):
            share(buffer, send, recv, far_peer(i), i, far_peer(i)).wait_recv()
            share_on(buffer, send, recv, i).start()

        each(1, chips, step)

    def share_sent(buffer, send, recv):
        share_near(buffer, send, recv).wait_send()

        def step(i):
            share_far(buffer, send, recv, i).wait_send()
            share_on(buffer, send, recv, i).wait_send()

        each(1, chips, step)

    def to_line(buffer, send, recv, line):
        return remote(
            buffer.at[z], buffer.at[z], send.at[line], recv.at[z], (me_h, line * group + r)
        )

    def from_line(buffer, send, recv, line):
        return remote(
            buffer.at[line],
            buffer.at[line],
            send.at[line],
            recv.at[line],
            (me_h, line * group + r),
        )

    def stat(buffer, send, recv, i):
        return remote(
            buffer.at[r], buffer.at[r], send.at[i], recv.at[r], (me_h, base + group_peer(i))
        )

    def stat_arrival(buffer, send, recv, i):
        src = group_peer(i)
        return remote(
            buffer.at[src], buffer.at[src], send.at[i], recv.at[src], (me_h, base + src)
        )

    def back(out, landing, send, recv, line):
        return remote(
            out.at[line], landing.at[z], send.at[line], recv.at[z], (me_h, line * group + r)
        )

    def back_arrival(out, landing, send, recv, line):
        return remote(
            out.at[line], landing.at[line], send.at[line], recv.at[line], (me_h, line * group + r)
        )

    def dq_near(j):
        there = 2 * j + 1 - core
        return remote(
            dq_out.at[there], dq_sib.at[j], s_send.at[j], s_recv.at[j], (me_h, base + sibling)
        )

    def dq_away(i):
        peer = far_peer(i)
        return remote(
            dq_far.at[lax.div(peer, 2)],
            dq_in.at[chip],
            dq_send.at[i],
            dq_recv.at[chip],
            (me_h, base + peer),
        )

    def dq_arrival(i):
        src = far_peer(i)
        return remote(
            dq_far.at[lax.div(src, 2)],
            dq_in.at[lax.div(src, 2)],
            dq_send.at[i],
            dq_recv.at[lax.div(src, 2)],
            (me_h, base + src),
        )

    barrier = pltpu.get_barrier_semaphore()

    def greet(device):
        pl.semaphore_signal(barrier, inc=1, device_id=device, device_id_type=MESH)

    each(1, heads, lambda i: greet((lax.rem(me_h + i, heads), me_c)))
    each(1, ctxs, lambda i: greet((me_h, lax.rem(me_c + i, ctxs))))

    loads = [
        pltpu.make_async_copy(slots_hbm, slots_in, in_sem.at[0]),
        pltpu.make_async_copy(spans_hbm, spans_in, in_sem.at[1]),
        pltpu.make_async_copy(q_hbm, qg.at[block(r), :], in_sem.at[2]),
        pltpu.make_async_copy(k_hbm, kb.at[z], in_sem.at[3]),
        pltpu.make_async_copy(v_hbm, vb.at[z], in_sem.at[4]),
    ]
    for h in range(heads):
        loads.append(
            pltpu.make_async_copy(
                t_hbm.at[:, h * DH : (h + 1) * DH], hop1_out.at[h, 0:trows, :], in_sem.at[5 + h]
            )
        )
    for load in loads:
        load.start()
    loads[0].wait()
    loads[1].wait()

    line16 = iota((16, trows), 0)
    slots = slots_in[...].astype(F32)
    spans = spans_in[...].astype(F32)
    meta = jnp.where(
        line16 == 0,
        slots,
        jnp.where(line16 == 1, spans[0:1], jnp.where(line16 == 2, spans[1:2], 0.0)),
    ).astype(BF16)
    place = jnp.bitwise_and(iota((trows, DH), 1), 63)
    pick = (place == iota((trows, DH), 0)).astype(F32).astype(BF16)
    meta = dot_nn(meta, pick)
    unused = (jnp.bitwise_and(iota((16, DH), 1), 63) >= trows) & (iota((16, DH), 0) == 0)
    meta = jnp.where(unused, -1.0, meta).astype(BF16)
    for h in range(heads):
        if trows < 48:
            hop1_out[h, trows:48, :] = jnp.zeros((48 - trows, DH), BF16)
        hop1_out[h, 48:64, :] = meta
    for load in loads[2:]:
        load.wait()

    pl.semaphore_wait(barrier, heads - 1 + ctxs - 1)

    each(1, heads, lambda i: hop1(i).start())
    hop1_in[me_h] = hop1_out[me_h]
    share_start(qg, q_send, q_recv)
    each(z + 1, lines, lambda line: to_line(kb, k_send, k_recv, line).start())
    each(1, heads, lambda i: hop1_arrival(i).wait_recv())

    kdepth = heads * 64
    teacher = hop1_in[...].reshape(kdepth, DH)
    eye = iota((64, DH), 0) == iota((64, DH), 1)
    ones = jnp.ones((DH, DH), BF16)
    firsts, lasts, codes = [], [], []
    lane1 = iota((1, DH), 1)
    for h in range(heads):
        tail = hop1_in[h, 48:64, :].astype(F32)
        firsts.append(jnp.where(eye, tail[1:2], 0.0).astype(BF16))
        lasts.append(jnp.where(eye, tail[2:3], 0.0).astype(BF16))
        codes.append(jnp.where(tail[0:1] < 0.0, -1.0, tail[0:1] + 128.0 * h))
    first = dot_nn(jnp.concatenate(firsts, axis=0), ones).astype(BF16)
    last = dot_nn(jnp.concatenate(lasts, axis=0), ones).astype(BF16)
    codes = [jnp.where(lane1 < 64, codes[h], codes[h + 1]) for h in range(0, heads, 2)]
    mine = lax.rem(me_c, 4) * 32

    def pack(step):
        row = iota((256, DH), 0)
        within = jnp.bitwise_and(row, 31)
        dest = lax.shift_right_logical(row, 5) + step * 8
        spot = lax.div(within, heads)
        head = within - spot * heads
        wanted = jnp.where(spot < CAP, dest * CAP + spot + 128 * head, -5).astype(F32)
        chosen = [(wanted == code).astype(F32).astype(BF16) for code in codes]
        chosen = jnp.concatenate(chosen, axis=1)
        moved = dot_nn(chosen, teacher).reshape(8, 32, DH)
        diagonal = (iota((256, DH), 1) == within + mine).astype(F32)
        lower = (dot_nn(chosen, first) * diagonal).reshape(8, 32, DH)
        upper = (dot_nn(chosen, last) * diagonal).reshape(8, 32, DH)
        lower = jnp.sum(lower, axis=1, keepdims=True)
        upper = jnp.sum(upper, axis=1, keepdims=True)
        line = iota((8, 8, DH), 1)
        tail = jnp.where(line == 0, lower, jnp.where(line == 1, upper, 0.0))
        message = jnp.concatenate([moved[:, 0:24, :], tail], axis=1)
        hop2_out[pl.ds(step * 8, 8)] = message.astype(BF16)

    each(0, ctxs // 8, pack)
    each(1, ctxs, lambda i: hop2(i).start())
    hop2_in[me_c] = hop2_out[me_c]
    each(z + 1, lines, lambda line: to_line(vb, v_send, v_recv, line).start())

    share_forward(qg, q_send, q_recv)

    def q_others(i):
        share(qg, q_send, q_recv, 2 * lax.rem(chip + i, chips) + 1 - core, 0, sibling).wait_recv()

    each(0, chips, q_others)
    each(0, z, lambda line: from_line(kb, k_send, k_recv, line).wait_recv())

    def transpose_keys(line):
        kt[line] = kb[line].astype(F32).T.astype(BF16)

    each(0, z + 1, transpose_keys)

    def scores_chunk(qc):
        queries = qg[pl.ds(pl.multiple_of(qc * CHUNK, CHUNK), CHUNK), :]

        def score(line, top):
            s = dot_nt(kb[line], queries)
            pt[line, qc] = s
            return jnp.maximum(top, jnp.max(s, axis=0, keepdims=True))

        top = lax.fori_loop(0, z, score, jnp.full((1, CHUNK), MASKED, F32))
        s = dot_nt(kb[z], queries)
        key_pos = iota((rows, CHUNK), 0) + r * rows
        query_pos = iota((rows, CHUNK), 1) + qc * CHUNK
        s = jnp.where(key_pos <= query_pos, s, MASKED)
        pt[z, qc] = s
        top = jnp.maximum(top, jnp.max(s, axis=0, keepdims=True))

        def weight(line, total):
            p = jnp.exp((pt[line, qc] - top) * scale)
            pt[line, qc] = p
            return total + jnp.sum(p, axis=0, keepdims=True)

        total = lax.fori_loop(0, z + 1, weight, jnp.zeros((1, CHUNK), F32))
        mrow[qc] = top * scale
        lse_st[r, qc] = top * scale + jnp.log(total)

    each(0, chunks, scores_chunk)
    each(1, group, lambda i: stat(lse_st, l_send, l_recv, i).start())
    each(1, group, lambda i: stat_arrival(lse_st, l_send, l_recv, i).wait_recv())

    def probs_chunk(qc):
        parts = lse_st[:, qc]
        top = jnp.max(parts, axis=0)
        lse = top + jnp.log(jnp.sum(jnp.exp(parts - top[None]), axis=0))
        fade = jnp.exp(mrow[qc] - lse)

        def fix(line):
            prob = pt[line, qc] * fade
            pt[line, qc] = prob
            p16[line, qc] = prob.astype(BF16)

        each(0, z + 1, fix)

    each(0, chunks, probs_chunk)

    each(1, ctxs, lambda i: hop2_arrival(i).wait_recv())
    token = iota((rows, DH), 0).astype(F32)

    def cover(step, total):
        four = hop2_in[pl.ds(step * 4, 4)]
        edges = jnp.sum(four[:, 16:32, :].astype(F32), axis=0)
        lower = edges[8:9]
        upper = edges[9:10]
        covered = jnp.where((token >= lower) & (token < upper), 1.0, 0.0).astype(BF16)
        return total + dot_nn(covered, four.reshape(4 * 32, DH))

    grad = lax.fori_loop(0, ctxs // 4, cover, jnp.zeros((rows, DH), F32))
    dog[block(r), :] = grad.astype(BF16)
    share_start(dog, do_send, do_recv)
    each(0, z, lambda line: from_line(vb, v_send, v_recv, line).wait_recv())

    def grad_probs(qc):
        grads = dog[pl.ds(pl.multiple_of(qc * CHUNK, CHUNK), CHUNK), :]

        def grad_prob(line, weighted):
            d = dot_nt(vb[line], grads)
            dp[line, qc] = d
            return weighted + jnp.sum(pt[line, qc] * d, axis=0, keepdims=True)

        del_st[r, qc] = lax.fori_loop(0, z + 1, grad_prob, jnp.zeros((1, CHUNK), F32))

    share(dog, do_send, do_recv, sibling, 0, sibling).wait_recv()
    grad_probs(chip)
    share_forward(dog, do_send, do_recv)

    def grad_others(i):
        there = lax.rem(chip + i, chips)
        share(dog, do_send, do_recv, 2 * there + 1 - core, 0, sibling).wait_recv()
        grad_probs(there)

    each(1, chips, grad_others)
    each(1, group, lambda i: stat(del_st, d_send, d_recv, i).start())

    def value_terms(line):
        total = jnp.zeros((rows, DH), F32)
        for qc in range(chunks):
            total += dot_nn(p16[line, qc], dog[qc * CHUNK : (qc + 1) * CHUNK, :])
        return total

    def earlier_values(line):
        dv_out[line] = value_terms(line).astype(BF16)
        back(dv_out, dv_in, dv_send, dv_recv, line).start()

    each(0, z, earlier_values)
    dv_own[...] = value_terms(z)

    each(1, group, lambda i: stat_arrival(del_st, d_send, d_recv, i).wait_recv())

    def deltas(qc):
        drow[qc] = jnp.sum(del_st[:, qc], axis=0)

    each(0, chunks, deltas)

    for b in range(group):
        dqa[b] = jnp.zeros((DH, rows), F32)

    def key_terms(line, last):
        key_sum = jnp.zeros((rows, DH), F32)
        for qc in range(chunks):
            dscore = (pt[line, qc] * (dp[line, qc] - drow[qc]) * scale).astype(BF16)
            key_sum += dot_nn(dscore, qg[qc * CHUNK : (qc + 1) * CHUNK, :])
            part = dot_nn(kt[line], dscore)
            for j in range(per_chunk):
                dqa[qc * per_chunk + j] += part[:, j * rows : (j + 1) * rows]
            if last:
                there = 2 * qc + 1 - core
                dq_out[there] = dqa[there].astype(BF16)
                dq_near(qc).start()
        return key_sum

    def earlier_keys(line):
        dk_out[line] = key_terms(line, False).astype(BF16)
        back(dk_out, dk_in, dk_send, dk_recv, line).start()

    each(0, z, earlier_keys)
    dk_own[...] = key_terms(z, True)

    def dq_join(i):
        here = lax.rem(chip + i, chips)
        dq_near(here).wait_recv()
        dq_far[here] = (dqa[2 * here + core] + dq_sib[here].astype(F32)).astype(BF16)
        dq_away(i).start()

    each(1, chips, dq_join)
    dq_near(chip).wait_recv()
    dq_total = dqa[r] + dq_sib[chip].astype(F32)

    def dv_add(line):
        back_arrival(dv_out, dv_in, dv_send, dv_recv, line).wait_recv()
        dv_own[...] += dv_in[line].astype(F32)

    each(z + 1, lines, dv_add)
    dv_ref[...] = dv_own[...].astype(BF16)

    def dk_add(line):
        back_arrival(dk_out, dk_in, dk_send, dk_recv, line).wait_recv()
        dk_own[...] += dk_in[line].astype(F32)

    each(z + 1, lines, dk_add)
    dk_ref[...] = dk_own[...].astype(BF16)

    def dq_add(i, total):
        dq_arrival(i).wait_recv()
        return total + dq_in[lax.div(far_peer(i), 2)].astype(F32)

    dq_total = lax.fori_loop(1, chips, dq_add, dq_total)
    dq_ref[...] = dq_total.T.astype(BF16)

    each(1, heads, lambda i: hop1(i).wait_send())
    each(1, ctxs, lambda i: hop2(i).wait_send())
    share_sent(qg, q_send, q_recv)
    share_sent(dog, do_send, do_recv)
    each(0, chips, lambda j: dq_near(j).wait_send())
    each(1, chips, lambda i: dq_away(i).wait_send())

    def stats_sent(i):
        stat(lse_st, l_send, l_recv, i).wait_send()
        stat(del_st, d_send, d_recv, i).wait_send()

    each(1, group, stats_sent)

    def lines_sent(line):
        to_line(kb, k_send, k_recv, line).wait_send()
        to_line(vb, v_send, v_recv, line).wait_send()

    each(z + 1, lines, lines_sent)

    def backs_sent(line):
        back(dv_out, dv_in, dv_send, dv_recv, line).wait_send()
        back(dk_out, dk_in, dk_send, dk_recv, line).wait_send()

    each(0, z, backs_sent)


def shards(heads, ctxs, group, queries, keys, values, teacher_rows, slots, spans):
    rows = queries.shape[0]
    trows = teacher_rows.shape[0]
    lines = ctxs // group
    chips = group // 2
    chunks = group * rows // CHUNK
    vm = pltpu.VMEM
    dma = pltpu.SemaphoreType.DMA
    scratch = [
        vm((1, trows), jnp.int32),
        vm((2, trows), jnp.int32),
        vm((heads, 64, DH), BF16),
        vm((heads, 64, DH), BF16),
        vm((ctxs, 32, DH), BF16),
        vm((ctxs, 32, DH), BF16),
        vm((group * rows, DH), BF16),
        vm((group * rows, DH), BF16),
        vm((lines, rows, DH), BF16),
        vm((lines, rows, DH), BF16),
        vm((lines, DH, rows), BF16),
        vm((lines, chunks, rows, CHUNK), F32),
        vm((lines, chunks, rows, CHUNK), BF16),
        vm((lines, chunks, rows, CHUNK), F32),
        vm((chunks, 1, CHUNK), F32),
        vm((group, chunks, 1, CHUNK), F32),
        vm((group, chunks, 1, CHUNK), F32),
        vm((chunks, 1, CHUNK), F32),
        vm((group, DH, rows), F32),
        vm((group, DH, rows), BF16),
        vm((chips, DH, rows), BF16),
        vm((chips, DH, rows), BF16),
        vm((chips, DH, rows), BF16),
        vm((lines, rows, DH), BF16),
        vm((lines, rows, DH), BF16),
        vm((rows, DH), F32),
        vm((lines, rows, DH), BF16),
        vm((lines, rows, DH), BF16),
        vm((rows, DH), F32),
        dma((5 + heads,)),
        dma((heads,)),
        dma((heads,)),
        dma((ctxs,)),
        dma((ctxs,)),
        dma((group,)),
        dma((group,)),
        dma((lines,)),
        dma((lines,)),
        dma((lines,)),
        dma((lines,)),
        dma((group,)),
        dma((group,)),
        dma((group,)),
        dma((group,)),
        dma((group,)),
        dma((group,)),
        dma((chips,)),
        dma((chips,)),
        dma((chips,)),
        dma((chips,)),
        dma((lines,)),
        dma((lines,)),
        dma((lines,)),
        dma((lines,)),
    ]
    out = jax.ShapeDtypeStruct((rows, DH), BF16)
    return pl.pallas_call(
        functools.partial(kernel, heads, ctxs, group),
        out_shape=(out, out, out),
        in_specs=[pl.BlockSpec(memory_space=pl.ANY)] * 6,
        out_specs=(pl.BlockSpec(memory_space=pltpu.VMEM),) * 3,
        scratch_shapes=scratch,
        compiler_params=pltpu.CompilerParams(
            collective_id=0, has_side_effects=True, vmem_limit_bytes=56 * 1024 * 1024
        ),
        name="attention_backward",
    )(queries, keys, values, teacher_rows, slots.reshape(1, trows), spans.T)


def solution(mesh):
    heads, ctxs = mesh.shape["head"], mesh.shape["ctx"]
    group = min(GROUP, ctxs // 2)
    return jax.shard_map(
        functools.partial(shards, heads, ctxs, group),
        mesh=mesh,
        in_specs=(
            P("ctx", "head"),
            P("ctx", "head"),
            P("ctx", "head"),
            P(("head", "ctx"), None),
            P(("head", "ctx")),
            P(("head", "ctx"), None),
        ),
        out_specs=(P("ctx", "head"), P("ctx", "head"), P("ctx", "head")),
        check_vma=False,
    )
```

```python
import functools
import math

import jax
import jax.numpy as jnp
from jax import lax
from jax.experimental import pallas as pl
from jax.experimental.pallas import tpu as pltpu
from jax.sharding import PartitionSpec as P

DH = 128
CAP = 3
GROUP = 8
CHUNK = 512
MASKED = -1e30
MESH = pl.DeviceIdType.MESH
F32 = jnp.float32
BF16 = jnp.bfloat16


def dot_nt(a, b):
    return lax.dot_general(a, b, (((1,), (1,)), ((), ())), preferred_element_type=F32)


def dot_nn(a, b):
    return lax.dot_general(a, b, (((1,), (0,)), ((), ())), preferred_element_type=F32)


def iota(shape, dim):
    return lax.broadcasted_iota(jnp.int32, shape, dim)


def kernel(heads, ctxs, group, *refs):
    (q_hbm, k_hbm, v_hbm, t_hbm, slots_hbm, spans_hbm, out_ref) = refs[:7]
    (slots_in, spans_in, hop1_out, hop1_in, hop2_out, hop2_in) = refs[7:13]
    (qg, dog, kb, vb, kt, pt, p16, dp, mrow, lse_st, del_st, drow) = refs[13:25]
    (dqa, dq_out, dq_sib, dq_far, dq_in) = refs[25:30]
    (dk_out, dk_in, dk_own, dv_out, dv_in, dv_own) = refs[30:36]
    (in_sem, h_send, h_recv, c_send, c_recv, q_send, q_recv, k_send, k_recv) = refs[36:45]
    (v_send, v_recv, do_send, do_recv, l_send, l_recv, d_send, d_recv) = refs[45:53]
    (s_send, s_recv, dq_send, dq_recv, dk_send, dk_recv, dv_send, dv_recv) = refs[53:61]
    me_h = lax.axis_index("head")
    me_c = lax.axis_index("ctx")
    z = lax.div(me_c, group)
    r = lax.rem(me_c, group)
    base = z * group
    core = lax.rem(r, 2)
    chip = lax.div(r, 2)
    chips = group // 2
    sibling = r + 1 - 2 * core
    rows = q_hbm.shape[0]
    trows = t_hbm.shape[0]
    lines = ctxs // group
    chunks = group * rows // CHUNK
    per_chunk = CHUNK // rows
    scale = 1.0 / math.sqrt(DH)

    def each(start, stop, f):
        def body(i, carry):
            f(i)
            return carry

        lax.fori_loop(start, stop, body, 0)

    def every(start, stop, f):
        for i in range(start, stop):
            f(i)

    def group_peer(i):
        return lax.rem(r + i, group)

    def far_peer(i):
        return lax.rem(r + 2 * i, group)

    def block(index):
        return pl.ds(pl.multiple_of(index * rows, rows), rows)

    def remote(src, dst, send, recv, device):
        return pltpu.make_async_remote_copy(
            src_ref=src,
            dst_ref=dst,
            send_sem=send,
            recv_sem=recv,
            device_id=device,
            device_id_type=MESH,
        )

    def hop1(i):
        peer = lax.rem(me_h + i, heads)
        return remote(hop1_out.at[peer], hop1_in.at[me_h], h_send, h_recv, (peer, me_c))

    def hop1_all():
        most = pl.ds(0, heads - 1)
        return remote(hop1_out.at[most], hop1_in.at[most], h_send, h_recv, (me_h, me_c))

    def hop2(i):
        peer = lax.rem(me_c + i, ctxs)
        return remote(hop2_out.at[peer], hop2_in.at[me_c], c_send, c_recv, (me_h, peer))

    def hop2_all():
        most = pl.ds(0, ctxs - 1)
        return remote(hop2_out.at[most], hop2_in.at[most], c_send, c_recv, (me_h, me_c))

    def share(buffer, send, recv, which, peer):
        here = buffer.at[block(which), :]
        return remote(here, here, send, recv.at[which], (me_h, base + peer))

    def share_far(buffer, send, recv, i):
        return share(buffer, send, recv, r, far_peer(i))

    def share_near(buffer, send, recv):
        return share(buffer, send, recv, r, sibling)

    def share_on(buffer, send, recv, i):
        return share(buffer, send, recv, far_peer(i), sibling)

    def share_start(buffer, send, recv):
        every(1, chips, lambda i: share_far(buffer, send, recv, i).start())
        share_near(buffer, send, recv).start()

    def share_forward(buffer, send, recv):
        def step(i):
            share(buffer, send, recv, far_peer(i), far_peer(i)).wait_recv()
            share_on(buffer, send, recv, i).start()

        every(1, chips, step)

    def share_sent(buffer, send, recv):
        most = buffer.at[pl.ds(0, (group - 1) * rows), :]
        remote(most, most, send, recv.at[0], (me_h, me_c)).wait_send()

    def to_line(buffer, send, recv, line):
        return remote(
            buffer.at[z], buffer.at[z], send.at[line], recv.at[z], (me_h, line * group + r)
        )

    def from_line(buffer, send, recv, line):
        return remote(
            buffer.at[line],
            buffer.at[line],
            send.at[line],
            recv.at[line],
            (me_h, line * group + r),
        )

    def stat(buffer, send, recv, i):
        return remote(buffer.at[r], buffer.at[r], send, recv, (me_h, base + group_peer(i)))

    def stat_all(buffer, send, recv):
        most = buffer.at[pl.ds(0, group - 1)]
        return remote(most, most, send, recv, (me_h, me_c))

    def back(out, landing, send, recv, line):
        return remote(
            out.at[line], landing.at[z], send.at[line], recv.at[z], (me_h, line * group + r)
        )

    def back_arrival(out, landing, send, recv, line):
        return remote(
            out.at[line], landing.at[line], send.at[line], recv.at[line], (me_h, line * group + r)
        )

    def dq_near(j):
        there = 2 * j + 1 - core
        return remote(
            dq_out.at[there], dq_sib.at[j], s_send.at[j], s_recv.at[j], (me_h, base + sibling)
        )

    def dq_away(i):
        peer = far_peer(i)
        return remote(
            dq_far.at[lax.div(peer, 2)],
            dq_in.at[chip],
            dq_send.at[i],
            dq_recv.at[chip],
            (me_h, base + peer),
        )

    def dq_arrival(i):
        src = far_peer(i)
        return remote(
            dq_far.at[lax.div(src, 2)],
            dq_in.at[lax.div(src, 2)],
            dq_send.at[i],
            dq_recv.at[lax.div(src, 2)],
            (me_h, base + src),
        )

    barrier = pltpu.get_barrier_semaphore()

    def greet(device):
        pl.semaphore_signal(barrier, inc=1, device_id=device, device_id_type=MESH)

    loads = [
        pltpu.make_async_copy(slots_hbm, slots_in, in_sem.at[0]),
        pltpu.make_async_copy(spans_hbm, spans_in, in_sem.at[1]),
        pltpu.make_async_copy(q_hbm, qg.at[block(r), :], in_sem.at[2]),
        pltpu.make_async_copy(k_hbm, kb.at[z], in_sem.at[3]),
        pltpu.make_async_copy(v_hbm, vb.at[z], in_sem.at[4]),
    ]
    for h in range(heads):
        loads.append(
            pltpu.make_async_copy(
                t_hbm.at[:, h * DH : (h + 1) * DH], hop1_out.at[h, 0:trows, :], in_sem.at[5 + h]
            )
        )
    for load in loads:
        load.start()
    every(1, heads, lambda i: greet((lax.rem(me_h + i, heads), me_c)))
    every(1, ctxs, lambda i: greet((me_h, lax.rem(me_c + i, ctxs))))
    loads[0].wait()
    loads[1].wait()

    line16 = iota((16, trows), 0)
    slots = slots_in[...].astype(F32)
    spans = spans_in[...].astype(F32)
    meta = jnp.where(
        line16 == 0,
        slots,
        jnp.where(line16 == 1, spans[0:1], jnp.where(line16 == 2, spans[1:2], 0.0)),
    ).astype(BF16)
    place = jnp.bitwise_and(iota((trows, DH), 1), 63)
    pick = (place == iota((trows, DH), 0)).astype(F32).astype(BF16)
    meta = dot_nn(meta, pick)
    unused = (jnp.bitwise_and(iota((16, DH), 1), 63) >= trows) & (iota((16, DH), 0) == 0)
    meta = jnp.where(unused, -1.0, meta).astype(BF16)
    for h in range(heads):
        if trows < 48:
            hop1_out[h, trows:48, :] = jnp.zeros((48 - trows, DH), BF16)
        hop1_out[h, 48:64, :] = meta
    for load in loads[2:]:
        load.wait()

    pl.semaphore_wait(barrier, heads - 1 + ctxs - 1)

    every(1, heads, lambda i: hop1(i).start())
    hop1_in[me_h] = hop1_out[me_h]
    share_start(qg, q_send, q_recv)
    each(z + 1, lines, lambda line: to_line(kb, k_send, k_recv, line).start())
    hop1_all().wait_recv()

    kdepth = heads * 64
    teacher = hop1_in[...].reshape(kdepth, DH)
    eye = iota((64, DH), 0) == iota((64, DH), 1)
    ones = jnp.ones((DH, DH), BF16)
    firsts, lasts, codes = [], [], []
    lane1 = iota((1, DH), 1)
    for h in range(heads):
        tail = hop1_in[h, 48:64, :].astype(F32)
        firsts.append(jnp.where(eye, tail[1:2], 0.0).astype(BF16))
        lasts.append(jnp.where(eye, tail[2:3], 0.0).astype(BF16))
        codes.append(jnp.where(tail[0:1] < 0.0, -1.0, tail[0:1] + 128.0 * h))
    first = dot_nn(jnp.concatenate(firsts, axis=0), ones).astype(BF16)
    last = dot_nn(jnp.concatenate(lasts, axis=0), ones).astype(BF16)
    codes = [jnp.where(lane1 < 64, codes[h], codes[h + 1]) for h in range(0, heads, 2)]
    mine = lax.rem(me_c, 4) * 32

    def pack(step):
        row = iota((256, DH), 0)
        within = jnp.bitwise_and(row, 31)
        dest = lax.shift_right_logical(row, 5) + step * 8
        spot = lax.div(within, heads)
        head = within - spot * heads
        wanted = jnp.where(spot < CAP, dest * CAP + spot + 128 * head, -5).astype(F32)
        chosen = [(wanted == code).astype(F32).astype(BF16) for code in codes]
        chosen = jnp.concatenate(chosen, axis=1)
        moved = dot_nn(chosen, teacher).reshape(8, 32, DH)
        diagonal = (iota((256, DH), 1) == within + mine).astype(F32)
        lower = (dot_nn(chosen, first) * diagonal).reshape(8, 32, DH)
        upper = (dot_nn(chosen, last) * diagonal).reshape(8, 32, DH)
        lower = jnp.sum(lower, axis=1, keepdims=True)
        upper = jnp.sum(upper, axis=1, keepdims=True)
        line = iota((8, 8, DH), 1)
        tail = jnp.where(line == 0, lower, jnp.where(line == 1, upper, 0.0))
        message = jnp.concatenate([moved[:, 0:24, :], tail], axis=1)
        hop2_out[pl.ds(step * 8, 8)] = message.astype(BF16)

    for step in range(ctxs // 8):
        pack(step)
    every(1, ctxs, lambda i: hop2(i).start())
    hop2_in[me_c] = hop2_out[me_c]

    each(z + 1, lines, lambda line: to_line(vb, v_send, v_recv, line).start())
    share_forward(qg, q_send, q_recv)

    def q_others(i):
        share(qg, q_send, q_recv, 2 * lax.rem(chip + i, chips) + 1 - core, sibling).wait_recv()

    every(0, chips, q_others)
    each(0, z, lambda line: from_line(kb, k_send, k_recv, line).wait_recv())

    def transpose_keys(line):
        kt[line] = kb[line].astype(F32).T.astype(BF16)

    each(0, z + 1, transpose_keys)

    def scores_chunk(qc):
        queries = qg[pl.ds(pl.multiple_of(qc * CHUNK, CHUNK), CHUNK), :]

        def score(line, top):
            s = dot_nt(kb[line], queries)
            pt[line, qc] = s
            return jnp.maximum(top, jnp.max(s, axis=0, keepdims=True))

        top = lax.fori_loop(0, z, score, jnp.full((1, CHUNK), MASKED, F32))
        s = dot_nt(kb[z], queries)
        key_pos = iota((rows, CHUNK), 0) + r * rows
        query_pos = iota((rows, CHUNK), 1) + qc * CHUNK
        s = jnp.where(key_pos <= query_pos, s, MASKED)
        pt[z, qc] = s
        top = jnp.maximum(top, jnp.max(s, axis=0, keepdims=True))

        def weight(line, total):
            p = jnp.exp((pt[line, qc] - top) * scale)
            pt[line, qc] = p
            return total + jnp.sum(p, axis=0, keepdims=True)

        total = lax.fori_loop(0, z + 1, weight, jnp.zeros((1, CHUNK), F32))
        mrow[qc] = top * scale
        lse_st[r, qc] = top * scale + jnp.log(total)

    each(0, chunks, scores_chunk)
    every(1, group, lambda i: stat(lse_st, l_send, l_recv, i).start())
    stat_all(lse_st, l_send, l_recv).wait_recv()

    def probs_chunk(qc):
        parts = lse_st[:, qc]
        top = jnp.max(parts, axis=0)
        lse = top + jnp.log(jnp.sum(jnp.exp(parts - top[None]), axis=0))
        fade = jnp.exp(mrow[qc] - lse)

        def fix(line):
            prob = pt[line, qc] * fade
            pt[line, qc] = prob
            p16[line, qc] = prob.astype(BF16)

        each(0, z + 1, fix)

    each(0, chunks, probs_chunk)

    hop2_all().wait_recv()
    token = iota((rows, DH), 0).astype(F32)

    def cover(step, total):
        four = hop2_in[pl.ds(step * 4, 4)]
        edges = jnp.sum(four[:, 16:32, :].astype(F32), axis=0)
        lower = edges[8:9]
        upper = edges[9:10]
        covered = jnp.where((token >= lower) & (token < upper), 1.0, 0.0).astype(BF16)
        return total + dot_nn(covered, four.reshape(4 * 32, DH))

    grad = jnp.zeros((rows, DH), F32)
    for step in range(ctxs // 4):
        grad = cover(step, grad)
    dog[block(r), :] = grad.astype(BF16)
    share_start(dog, do_send, do_recv)

    share_forward(dog, do_send, do_recv)

    def do_others(i):
        share(dog, do_send, do_recv, 2 * lax.rem(chip + i, chips) + 1 - core, sibling).wait_recv()

    every(0, chips, do_others)

    def value_terms(line):
        total = jnp.zeros((rows, DH), F32)
        for qc in range(chunks):
            total += dot_nn(p16[line, qc], dog[qc * CHUNK : (qc + 1) * CHUNK, :])
        return total

    def earlier_values(line):
        dv_out[line] = value_terms(line).astype(BF16)
        back(dv_out, dv_in, dv_send, dv_recv, line).start()

    each(0, z, earlier_values)
    dv_own[...] = value_terms(z)

    def grad_probs(line):
        sums = []
        for qc in range(chunks):
            d = dot_nt(vb[line], dog[qc * CHUNK : (qc + 1) * CHUNK, :])
            dp[line, qc] = d
            sums.append(jnp.sum(pt[line, qc] * d, axis=0, keepdims=True))
        return sums

    sums = grad_probs(z)
    for qc in range(chunks):
        del_st[r, qc] = sums[qc]

    def earlier_probs(i):
        line = z - i
        from_line(vb, v_send, v_recv, line).wait_recv()
        sums = grad_probs(line)
        for qc in range(chunks):
            del_st[r, qc] += sums[qc]

    each(1, z + 1, earlier_probs)
    every(1, group, lambda i: stat(del_st, d_send, d_recv, i).start())

    hop1_all().wait_send()
    hop2_all().wait_send()
    share_sent(qg, q_send, q_recv)
    share_sent(dog, do_send, do_recv)
    stat_all(lse_st, l_send, l_recv).wait_send()

    def lines_sent(line):
        to_line(kb, k_send, k_recv, line).wait_send()
        to_line(vb, v_send, v_recv, line).wait_send()

    each(z + 1, lines, lines_sent)

    stat_all(del_st, d_send, d_recv).wait_recv()
    stat_all(del_st, d_send, d_recv).wait_send()

    def deltas(qc):
        drow[qc] = jnp.sum(del_st[:, qc], axis=0)

    each(0, chunks, deltas)

    for b in range(group):
        dqa[b] = jnp.zeros((DH, rows), F32)

    def key_terms(line, last):
        key_sum = jnp.zeros((rows, DH), F32)
        for qc in range(chunks):
            dscore = (pt[line, qc] * (dp[line, qc] - drow[qc]) * scale).astype(BF16)
            key_sum += dot_nn(dscore, qg[qc * CHUNK : (qc + 1) * CHUNK, :])
            part = dot_nn(kt[line], dscore)
            for j in range(per_chunk):
                dqa[qc * per_chunk + j] += part[:, j * rows : (j + 1) * rows]
            if last:
                there = 2 * qc + 1 - core
                dq_out[there] = dqa[there].astype(BF16)
                dq_near(qc).start()
        return key_sum

    def earlier_keys(line):
        dk_out[line] = key_terms(line, False).astype(BF16)
        back(dk_out, dk_in, dk_send, dk_recv, line).start()

    each(0, z, earlier_keys)
    dk_own[...] = key_terms(z, True)

    def dq_join(i):
        here = lax.rem(chip + i, chips)
        dq_near(here).wait_recv()
        dq_far[here] = (dqa[2 * here + core] + dq_sib[here].astype(F32)).astype(BF16)
        dq_away(i).start()

    each(1, chips, dq_join)
    dq_near(chip).wait_recv()
    dq_total = dqa[r] + dq_sib[chip].astype(F32)

    def dv_add(line):
        back_arrival(dv_out, dv_in, dv_send, dv_recv, line).wait_recv()
        dv_own[...] += dv_in[line].astype(F32)

    each(z + 1, lines, dv_add)
    out_ref[2] = dv_own[...].astype(BF16)

    def dk_add(line):
        back_arrival(dk_out, dk_in, dk_send, dk_recv, line).wait_recv()
        dk_own[...] += dk_in[line].astype(F32)

    each(z + 1, lines, dk_add)
    out_ref[1] = dk_own[...].astype(BF16)

    def dq_add(i, total):
        dq_arrival(i).wait_recv()
        return total + dq_in[lax.div(far_peer(i), 2)].astype(F32)

    dq_total = lax.fori_loop(1, chips, dq_add, dq_total)
    out_ref[0] = dq_total.T.astype(BF16)

    each(0, chips, lambda j: dq_near(j).wait_send())
    each(1, chips, lambda i: dq_away(i).wait_send())

    def backs_sent(line):
        back(dv_out, dv_in, dv_send, dv_recv, line).wait_send()
        back(dk_out, dk_in, dk_send, dk_recv, line).wait_send()

    each(0, z, backs_sent)


def shards(heads, ctxs, group, queries, keys, values, teacher_rows, slots, spans):
    rows = queries.shape[0]
    trows = teacher_rows.shape[0]
    lines = ctxs // group
    chips = group // 2
    chunks = group * rows // CHUNK
    vm = pltpu.VMEM
    dma = pltpu.SemaphoreType.DMA
    scratch = [
        vm((1, trows), jnp.int32),
        vm((2, trows), jnp.int32),
        vm((heads, 64, DH), BF16),
        vm((heads, 64, DH), BF16),
        vm((ctxs, 32, DH), BF16),
        vm((ctxs, 32, DH), BF16),
        vm((group * rows, DH), BF16),
        vm((group * rows, DH), BF16),
        vm((lines, rows, DH), BF16),
        vm((lines, rows, DH), BF16),
        vm((lines, DH, rows), BF16),
        vm((lines, chunks, rows, CHUNK), F32),
        vm((lines, chunks, rows, CHUNK), BF16),
        vm((lines, chunks, rows, CHUNK), F32),
        vm((chunks, 1, CHUNK), F32),
        vm((group, chunks, 1, CHUNK), F32),
        vm((group, chunks, 1, CHUNK), F32),
        vm((chunks, 1, CHUNK), F32),
        vm((group, DH, rows), F32),
        vm((group, DH, rows), BF16),
        vm((chips, DH, rows), BF16),
        vm((chips, DH, rows), BF16),
        vm((chips, DH, rows), BF16),
        vm((lines, rows, DH), BF16),
        vm((lines, rows, DH), BF16),
        vm((rows, DH), F32),
        vm((lines, rows, DH), BF16),
        vm((lines, rows, DH), BF16),
        vm((rows, DH), F32),
        dma((5 + heads,)),
        dma,
        dma,
        dma,
        dma,
        dma,
        dma((group,)),
        dma((lines,)),
        dma((lines,)),
        dma((lines,)),
        dma((lines,)),
        dma,
        dma((group,)),
        dma,
        dma,
        dma,
        dma,
        dma((chips,)),
        dma((chips,)),
        dma((chips,)),
        dma((chips,)),
        dma((lines,)),
        dma((lines,)),
        dma((lines,)),
        dma((lines,)),
    ]
    out = pl.pallas_call(
        functools.partial(kernel, heads, ctxs, group),
        out_shape=jax.ShapeDtypeStruct((3, rows, DH), BF16),
        in_specs=[pl.BlockSpec(memory_space=pl.ANY)] * 6,
        out_specs=pl.BlockSpec(memory_space=pltpu.VMEM),
        scratch_shapes=scratch,
        compiler_params=pltpu.CompilerParams(
            collective_id=0, has_side_effects=True, vmem_limit_bytes=56 * 1024 * 1024
        ),
        name="attention_backward",
    )(queries, keys, values, teacher_rows, slots.reshape(1, trows), spans.T)
    return out[0], out[1], out[2]


def solution(mesh):
    heads, ctxs = mesh.shape["head"], mesh.shape["ctx"]
    group = min(GROUP, ctxs // 2)
    return jax.shard_map(
        functools.partial(shards, heads, ctxs, group),
        mesh=mesh,
        in_specs=(
            P("ctx", "head"),
            P("ctx", "head"),
            P("ctx", "head"),
            P(("head", "ctx"), None),
            P(("head", "ctx")),
            P(("head", "ctx"), None),
        ),
        out_specs=(P("ctx", "head"), P("ctx", "head"), P("ctx", "head")),
        check_vma=False,
    )
```

```python
import functools
import math

import jax
import jax.numpy as jnp
from jax import lax
from jax.experimental import pallas as pl
from jax.experimental.pallas import tpu as pltpu
from jax.sharding import PartitionSpec as P

DH = 128
CAP = 3
GROUP = 8
CHUNK = 512
MASKED = -1e30
MESH = pl.DeviceIdType.MESH
F32 = jnp.float32
BF16 = jnp.bfloat16


def dot_nt(a, b):
    return lax.dot_general(a, b, (((1,), (1,)), ((), ())), preferred_element_type=F32)


def dot_nn(a, b):
    return lax.dot_general(a, b, (((1,), (0,)), ((), ())), preferred_element_type=F32)


def iota(shape, dim):
    return lax.broadcasted_iota(jnp.int32, shape, dim)


def kernel(heads, ctxs, group, *refs):
    (q_hbm, k_hbm, v_hbm, t_hbm, slots_hbm, spans_hbm, out_ref) = refs[:7]
    (slots_in, spans_in, hop1_in, hop2_out, hop2_in) = refs[7:12]
    (qg, dog, kb, vb, kt, pt, p16, dp, mrow, lse_st, del_st, drow) = refs[12:24]
    (dqa, dq_out, dq_in, dk_out, dk_in, dk_own, dv_out, dv_in, dv_own) = refs[24:33]
    (dk_part, dk_land, dk_keep, dv_part, dv_land, dv_keep, out_v) = refs[33:40]
    (in_sem, h_send, h_recv, c_send, c_recv, q_send, q_recv, do_send, do_recv) = refs[40:49]
    (l_send, l_recv, d_send, d_recv, dq_send, dq_recv) = refs[49:55]
    (k_send, k_recv, v_send, v_recv, kn_send, kn_recv, vn_send, vn_recv) = refs[55:63]
    (pv_send, pv_recv, pk_send, pk_recv, dk_send, dk_recv, dv_send, dv_recv) = refs[63:]
    me_h = lax.axis_index("head")
    me_c = lax.axis_index("ctx")
    z = lax.div(me_c, group)
    r = lax.rem(me_c, group)
    base = z * group
    core = lax.rem(r, 2)
    chip = lax.div(r, 2)
    chips = group // 2
    sibling = r + 1 - 2 * core
    rows = q_hbm.shape[0]
    trows = t_hbm.shape[0]
    lines = ctxs // group
    chunks = chips * rows // CHUNK
    per_chunk = CHUNK // rows
    other = 1 - core
    scale = 1.0 / math.sqrt(DH)

    def each(start, stop, f):
        def body(i, carry):
            f(i)
            return carry

        lax.fori_loop(start, stop, body, 0)

    def every(start, stop, f):
        for i in range(start, stop):
            f(i)

    def mate(i):
        return lax.rem(chip + i, chips)

    def device(of_chip):
        return (me_h, base + 2 * of_chip + core)

    def block(index):
        return pl.ds(pl.multiple_of(index * rows, rows), rows)

    def remote(src, dst, send, recv, device):
        return pltpu.make_async_remote_copy(
            src_ref=src,
            dst_ref=dst,
            send_sem=send,
            recv_sem=recv,
            device_id=device,
            device_id_type=MESH,
        )

    def hop1(i):
        peer = lax.rem(me_h + i, heads)
        columns = pl.ds(pl.multiple_of(peer * DH, DH), DH)
        return [
            remote(src, dst, h_send, sem, (peer, me_c))
            for src, dst, sem in (
                (slots_hbm, slots_in.at[me_h], h_recv.at[0]),
                (spans_hbm, spans_in.at[me_h], h_recv.at[1]),
                (t_hbm.at[:, columns], hop1_in.at[me_h, pl.ds(0, trows), :], h_recv.at[2]),
            )
        ]

    def hop1_all():
        most = pl.ds(0, heads - 1)
        here = (
            slots_in.at[most],
            spans_in.at[most],
            hop1_in.at[most, pl.ds(0, trows), :],
        )
        return [
            remote(ref, ref, h_send, h_recv.at[j], (me_h, me_c)) for j, ref in enumerate(here)
        ]

    def hop2(i):
        peer = lax.rem(me_c + i, ctxs)
        return remote(hop2_out.at[peer], hop2_in.at[me_c], c_send, c_recv, (me_h, peer))

    def hop2_all():
        most = pl.ds(0, ctxs - 1)
        return remote(hop2_out.at[most], hop2_in.at[most], c_send, c_recv, (me_h, me_c))

    def share_start(buffer, send, recv):
        here = buffer.at[block(chip), :]
        every(1, chips, lambda i: remote(here, here, send, recv, device(mate(i))).start())

    def share_all(buffer, send, recv):
        most = buffer.at[pl.ds(0, (chips - 1) * rows), :]
        return remote(most, most, send, recv, (me_h, me_c))

    def to_line(buffer, send, recv, line):
        here = buffer.at[z, core]
        return remote(here, here, send.at[line], recv.at[z], (me_h, line * group + r))

    def from_line(buffer, send, recv, line):
        here = buffer.at[line, core]
        return remote(here, here, send.at[line], recv.at[line], (me_h, line * group + r))

    def near(buffer, send, recv, line):
        here = buffer.at[line, core]
        return remote(here, here, send.at[line], recv.at[line], (me_h, base + sibling))

    def near_arrival(buffer, send, recv, line):
        here = buffer.at[line, other]
        return remote(here, here, send.at[line], recv.at[line], (me_h, base + sibling))

    def forward(buffer, send, recv, near_send, near_recv):
        def step(line):
            from_line(buffer, send, recv, line).wait_recv()
            near(buffer, near_send, near_recv, line).start()

        each(0, z, step)

    def part(out, landing, send, recv, line):
        return remote(
            out.at[line], landing.at[line], send.at[line], recv.at[line], (me_h, base + sibling)
        )

    def stat(buffer, send, recv, i):
        return remote(buffer.at[chip], buffer.at[chip], send, recv, device(mate(i)))

    def stat_all(buffer, send, recv):
        most = buffer.at[pl.ds(0, chips - 1)]
        return remote(most, most, send, recv, (me_h, me_c))

    def back(out, landing, send, recv, line):
        return remote(
            out.at[line], landing.at[z], send.at[line], recv.at[z], (me_h, line * group + r)
        )

    def back_arrival(out, landing, send, recv, line):
        return remote(
            out.at[line], landing.at[line], send.at[line], recv.at[line], (me_h, line * group + r)
        )

    def dq_away(i):
        return remote(
            dq_out.at[mate(i)], dq_in.at[chip], dq_send.at[i], dq_recv.at[chip], device(mate(i))
        )

    def dq_arrival(i):
        return remote(
            dq_out.at[mate(i)], dq_in.at[mate(i)], dq_send.at[i], dq_recv.at[mate(i)], device(mate(i))
        )

    def out_copy(which):
        return pltpu.make_async_copy(out_v.at[which], out_ref.at[which], in_sem.at[6 + which])

    barrier = pltpu.get_barrier_semaphore()

    def greet(device):
        pl.semaphore_signal(barrier, inc=1, device_id=device, device_id_type=MESH)

    loads = [
        pltpu.make_async_copy(q_hbm, qg.at[block(chip), :], in_sem.at[0]),
        pltpu.make_async_copy(k_hbm, kb.at[z, core], in_sem.at[1]),
        pltpu.make_async_copy(v_hbm, vb.at[z, core], in_sem.at[2]),
        pltpu.make_async_copy(slots_hbm, slots_in.at[me_h], in_sem.at[3]),
        pltpu.make_async_copy(spans_hbm, spans_in.at[me_h], in_sem.at[4]),
        pltpu.make_async_copy(
            t_hbm.at[:, pl.ds(pl.multiple_of(me_h * DH, DH), DH)],
            hop1_in.at[me_h, pl.ds(0, trows), :],
            in_sem.at[5],
        ),
    ]
    every(1, heads, lambda i: greet((lax.rem(me_h + i, heads), me_c)))
    every(1, ctxs, lambda i: greet((me_h, lax.rem(me_c + i, ctxs))))
    for load in loads:
        load.start()
    hop1_in[:, trows:64, :] = jnp.zeros((heads, 64 - trows, DH), BF16)

    pl.semaphore_wait(barrier, heads - 1 + ctxs - 1)

    def hop1_start(i):
        for copy in hop1(i):
            copy.start()

    every(1, heads, hop1_start)
    for load in loads:
        load.wait()
    share_start(qg, q_send, q_recv)
    each(z + 1, lines, lambda line: to_line(kb, k_send, k_recv, line).start())
    near(kb, kn_send, kn_recv, z).start()
    near(vb, vn_send, vn_recv, z).start()
    for copy in hop1_all():
        copy.wait_recv()

    kdepth = heads * 64
    teacher = hop1_in[...].reshape(kdepth, DH)
    eye = iota((64, trows), 0) == iota((64, trows), 1)
    ones = jnp.ones((trows, DH), BF16)
    firsts, lasts = [], []
    slots = jnp.zeros((16, trows), F32)
    for h in range(heads):
        spans = spans_in[h].astype(F32)
        firsts.append(jnp.where(eye, spans[0:1], 0.0).astype(BF16))
        lasts.append(jnp.where(eye, spans[1:2], 0.0).astype(BF16))
        slots = jnp.where(iota((16, trows), 0) == h, slots_in[h].astype(F32), slots)
    first = dot_nn(jnp.concatenate(firsts, axis=0), ones).astype(BF16)
    last = dot_nn(jnp.concatenate(lasts, axis=0), ones).astype(BF16)
    place = jnp.bitwise_and(iota((trows, DH), 1), 63)
    pick = (place == iota((trows, DH), 0)).astype(F32).astype(BF16)
    slots = dot_nn(slots.astype(BF16), pick) + 128.0 * iota((16, DH), 0).astype(F32)
    unused = jnp.bitwise_and(iota((16, DH), 1), 63) >= trows
    slots = jnp.where(unused, -1.0, slots)
    left = iota((1, DH), 1) < 64
    codes = [
        jnp.where(left, slots[h : h + 1], slots[h + 1 : h + 2]) for h in range(0, heads, 2)
    ]
    mine = lax.rem(me_c, 4) * 32

    def pack(step):
        row = iota((256, DH), 0)
        within = jnp.bitwise_and(row, 31)
        dest = lax.shift_right_logical(row, 5) + step * 8
        spot = lax.div(within, heads)
        head = within - spot * heads
        wanted = jnp.where(spot < CAP, dest * CAP + spot + 128 * head, -5).astype(F32)
        chosen = [(wanted == code).astype(F32).astype(BF16) for code in codes]
        chosen = jnp.concatenate(chosen, axis=1)
        moved = dot_nn(chosen, teacher).reshape(8, 32, DH)
        diagonal = (iota((256, DH), 1) == within + mine).astype(F32)
        lower = (dot_nn(chosen, first) * diagonal).reshape(8, 32, DH)
        upper = (dot_nn(chosen, last) * diagonal).reshape(8, 32, DH)
        lower = jnp.sum(lower, axis=1, keepdims=True)
        upper = jnp.sum(upper, axis=1, keepdims=True)
        line = iota((8, 8, DH), 1)
        tail = jnp.where(line == 0, lower, jnp.where(line == 1, upper, 0.0))
        message = jnp.concatenate([moved[:, 0:24, :], tail], axis=1)
        hop2_out[pl.ds(step * 8, 8)] = message.astype(BF16)

    for step in range(ctxs // 8):
        pack(step)
    every(1, ctxs, lambda i: hop2(i).start())
    hop2_in[me_c] = hop2_out[me_c]

    each(z + 1, lines, lambda line: to_line(vb, v_send, v_recv, line).start())
    forward(kb, k_send, k_recv, kn_send, kn_recv)
    share_all(qg, q_send, q_recv).wait_recv()

    def transpose_keys(line):
        near_arrival(kb, kn_send, kn_recv, line).wait_recv()
        for side in range(2):
            kt[line, side] = kb[line, side].astype(F32).T.astype(BF16)

    each(0, z + 1, transpose_keys)

    def scores_chunk(qc):
        queries = qg[pl.ds(pl.multiple_of(qc * CHUNK, CHUNK), CHUNK), :]

        def score(line, top):
            for side in range(2):
                s = dot_nt(kb[line, side], queries)
                pt[line, side, qc] = s
                top = jnp.maximum(top, jnp.max(s, axis=0, keepdims=True))
            return top

        top = lax.fori_loop(0, z, score, jnp.full((1, CHUNK), MASKED, F32))
        place = iota((rows, CHUNK), 1) + qc * CHUNK
        query_pos = place + (lax.div(place, rows) + core) * rows
        for side in range(2):
            s = dot_nt(kb[z, side], queries)
            key_pos = iota((rows, CHUNK), 0) + (2 * chip + side) * rows
            s = jnp.where(key_pos <= query_pos, s, MASKED)
            pt[z, side, qc] = s
            top = jnp.maximum(top, jnp.max(s, axis=0, keepdims=True))

        def weight(line, total):
            for side in range(2):
                p = jnp.exp((pt[line, side, qc] - top) * scale)
                pt[line, side, qc] = p
                total = total + jnp.sum(p, axis=0, keepdims=True)
            return total

        total = lax.fori_loop(0, z + 1, weight, jnp.zeros((1, CHUNK), F32))
        mrow[qc] = top * scale
        lse_st[chip, qc] = top * scale + jnp.log(total)

    each(0, chunks, scores_chunk)
    every(1, chips, lambda i: stat(lse_st, l_send, l_recv, i).start())
    stat_all(lse_st, l_send, l_recv).wait_recv()

    def probs_chunk(qc):
        parts = lse_st[:, qc]
        top = jnp.max(parts, axis=0)
        lse = top + jnp.log(jnp.sum(jnp.exp(parts - top[None]), axis=0))
        fade = jnp.exp(mrow[qc] - lse)

        def fix(line):
            for side in range(2):
                prob = pt[line, side, qc] * fade
                pt[line, side, qc] = prob
                p16[line, side, qc] = prob.astype(BF16)

        each(0, z + 1, fix)

    each(0, chunks, probs_chunk)

    hop2_all().wait_recv()
    token = iota((rows, DH), 0).astype(F32)

    def cover(step, total):
        four = hop2_in[pl.ds(step * 4, 4)]
        edges = jnp.sum(four[:, 16:32, :].astype(F32), axis=0)
        lower = edges[8:9]
        upper = edges[9:10]
        covered = jnp.where((token >= lower) & (token < upper), 1.0, 0.0).astype(BF16)
        return total + dot_nn(covered, four.reshape(4 * 32, DH))

    grad = jnp.zeros((rows, DH), F32)
    for step in range(ctxs // 4):
        grad = cover(step, grad)
    dog[block(chip), :] = grad.astype(BF16)
    share_start(dog, do_send, do_recv)

    forward(vb, v_send, v_recv, vn_send, vn_recv)
    share_all(dog, do_send, do_recv).wait_recv()

    def value_terms(line, side):
        total = jnp.zeros((rows, DH), F32)
        for qc in range(chunks):
            total += dot_nn(p16[line, side, qc], dog[qc * CHUNK : (qc + 1) * CHUNK, :])
        return total

    def value_parts(line):
        dv_part[line] = value_terms(line, other).astype(BF16)
        part(dv_part, dv_land, pv_send, pv_recv, line).start()
        dv_keep[line] = value_terms(line, core)

    def value_join(line):
        part(dv_part, dv_land, pv_send, pv_recv, line).wait_recv()
        dv_out[line] = (dv_keep[line] + dv_land[line].astype(F32)).astype(BF16)
        back(dv_out, dv_in, dv_send, dv_recv, line).start()

    each(0, z + 1, value_parts)
    each(0, z, value_join)

    def grad_probs(line, sums):
        for side in range(2):
            for qc in range(chunks):
                d = dot_nt(vb[line, side], dog[qc * CHUNK : (qc + 1) * CHUNK, :])
                dp[line, side, qc] = d
                here = jnp.sum(pt[line, side, qc] * d, axis=0, keepdims=True)
                sums[qc] = here if sums[qc] is None else sums[qc] + here
        return sums

    near_arrival(vb, vn_send, vn_recv, z).wait_recv()
    sums = grad_probs(z, [None] * chunks)
    for qc in range(chunks):
        del_st[chip, qc] = sums[qc]

    def earlier_probs(i):
        line = z - i
        near_arrival(vb, vn_send, vn_recv, line).wait_recv()
        sums = grad_probs(line, [None] * chunks)
        for qc in range(chunks):
            del_st[chip, qc] += sums[qc]

    each(1, z + 1, earlier_probs)
    every(1, chips, lambda i: stat(del_st, d_send, d_recv, i).start())

    for copy in hop1_all():
        copy.wait_send()
    hop2_all().wait_send()
    share_all(qg, q_send, q_recv).wait_send()
    share_all(dog, do_send, do_recv).wait_send()
    stat_all(lse_st, l_send, l_recv).wait_send()

    def lines_sent(line):
        to_line(kb, k_send, k_recv, line).wait_send()
        to_line(vb, v_send, v_recv, line).wait_send()

    each(z + 1, lines, lines_sent)

    def nears_sent(line):
        near(kb, kn_send, kn_recv, line).wait_send()
        near(vb, vn_send, vn_recv, line).wait_send()
        part(dv_part, dv_land, pv_send, pv_recv, line).wait_send()

    each(0, z + 1, nears_sent)
    for j in range(chips):
        dqa[j] = jnp.zeros((DH, rows), F32)

    stat_all(del_st, d_send, d_recv).wait_recv()
    stat_all(del_st, d_send, d_recv).wait_send()

    def deltas(qc):
        drow[qc] = jnp.sum(del_st[:, qc], axis=0)

    each(0, chunks, deltas)

    def dscores(line, side):
        for qc in range(chunks):
            dscore = (pt[line, side, qc] * (dp[line, side, qc] - drow[qc]) * scale).astype(BF16)
            p16[line, side, qc] = dscore
            terms = dot_nn(kt[line, side], dscore)
            for j in range(per_chunk):
                dqa[qc * per_chunk + j] += terms[:, j * rows : (j + 1) * rows]

    def key_terms(line, side):
        total = jnp.zeros((rows, DH), F32)
        for qc in range(chunks):
            total += dot_nn(p16[line, side, qc], qg[qc * CHUNK : (qc + 1) * CHUNK, :])
        return total

    def key_parts(line):
        dk_part[line] = key_terms(line, other).astype(BF16)
        part(dk_part, dk_land, pk_send, pk_recv, line).start()
        dk_keep[line] = key_terms(line, core)

    def key_sum(line):
        part(dk_part, dk_land, pk_send, pk_recv, line).wait_recv()
        return dk_keep[line] + dk_land[line].astype(F32)

    def key_join(line):
        dk_out[line] = key_sum(line).astype(BF16)
        back(dk_out, dk_in, dk_send, dk_recv, line).start()

    def earlier_keys(line):
        dscores(line, other)
        dscores(line, core)
        key_parts(line)
        pl.when(line > 0)(lambda: key_join(line - 1))

    each(0, z, earlier_keys)
    dscores(z, other)
    dscores(z, core)
    dq_out[...] = dqa[...].astype(BF16)
    every(1, chips, lambda i: dq_away(i).start())
    pl.when(z > 0)(lambda: key_join(z - 1))
    key_parts(z)

    part(dv_part, dv_land, pv_send, pv_recv, z).wait_recv()
    dv_own[...] = dv_keep[z] + dv_land[z].astype(F32)

    def dv_add(line):
        back_arrival(dv_out, dv_in, dv_send, dv_recv, line).wait_recv()
        dv_own[...] += dv_in[line].astype(F32)

    each(z + 1, lines, dv_add)
    out_v[2] = dv_own[...].astype(BF16)
    out_copy(2).start()
    dk_own[...] = key_sum(z)

    def dk_add(line):
        back_arrival(dk_out, dk_in, dk_send, dk_recv, line).wait_recv()
        dk_own[...] += dk_in[line].astype(F32)

    each(z + 1, lines, dk_add)
    out_v[1] = dk_own[...].astype(BF16)
    out_copy(1).start()

    def dq_add(i, total):
        dq_arrival(i).wait_recv()
        return total + dq_in[mate(i)].astype(F32)

    dq_total = lax.fori_loop(1, chips, dq_add, dqa[chip])
    out_v[0] = dq_total.T.astype(BF16)
    out_copy(0).start()

    every(1, chips, lambda i: dq_away(i).wait_send())
    each(0, z + 1, lambda line: part(dk_part, dk_land, pk_send, pk_recv, line).wait_send())

    def backs_sent(line):
        back(dv_out, dv_in, dv_send, dv_recv, line).wait_send()
        back(dk_out, dk_in, dk_send, dk_recv, line).wait_send()

    each(0, z, backs_sent)
    for which in range(3):
        out_copy(which).wait()


def shards(heads, ctxs, group, queries, keys, values, teacher_rows, slots, spans):
    rows = queries.shape[0]
    trows = teacher_rows.shape[0]
    lines = ctxs // group
    chips = group // 2
    chunks = chips * rows // CHUNK
    vm = pltpu.VMEM
    dma = pltpu.SemaphoreType.DMA
    parts = [vm((lines, rows, DH), BF16), vm((lines, rows, DH), BF16)]
    scratch = [
        vm((heads, 1, trows), jnp.int32),
        vm((heads, 2, trows), jnp.int32),
        vm((heads, 64, DH), BF16),
        vm((ctxs, 32, DH), BF16),
        vm((ctxs, 32, DH), BF16),
        vm((chips * rows, DH), BF16),
        vm((chips * rows, DH), BF16),
        vm((lines, 2, rows, DH), BF16),
        vm((lines, 2, rows, DH), BF16),
        vm((lines, 2, DH, rows), BF16),
        vm((lines, 2, chunks, rows, CHUNK), F32),
        vm((lines, 2, chunks, rows, CHUNK), BF16),
        vm((lines, 2, chunks, rows, CHUNK), F32),
        vm((chunks, 1, CHUNK), F32),
        vm((chips, chunks, 1, CHUNK), F32),
        vm((chips, chunks, 1, CHUNK), F32),
        vm((chunks, 1, CHUNK), F32),
        vm((chips, DH, rows), F32),
        vm((chips, DH, rows), BF16),
        vm((chips, DH, rows), BF16),
        *parts,
        vm((rows, DH), F32),
        *parts,
        vm((rows, DH), F32),
        *parts,
        vm((lines, rows, DH), F32),
        *parts,
        vm((lines, rows, DH), F32),
        vm((3, rows, DH), BF16),
        dma((9,)),
        dma,
        dma((3,)),
        *([dma] * 10),
        dma((chips,)),
        dma((chips,)),
        *([dma((lines,))] * 16),
    ]
    out = pl.pallas_call(
        functools.partial(kernel, heads, ctxs, group),
        out_shape=jax.ShapeDtypeStruct((3, rows, DH), BF16),
        in_specs=[pl.BlockSpec(memory_space=pl.ANY)] * 6,
        out_specs=pl.BlockSpec(memory_space=pl.ANY),
        scratch_shapes=scratch,
        compiler_params=pltpu.CompilerParams(
            collective_id=0, has_side_effects=True, vmem_limit_bytes=56 * 1024 * 1024
        ),
        name="attention_backward",
    )(queries, keys, values, teacher_rows, slots.reshape(1, trows), spans.T)
    return out[0], out[1], out[2]


def solution(mesh):
    heads, ctxs = mesh.shape["head"], mesh.shape["ctx"]
    group = min(GROUP, ctxs // 2)
    return jax.shard_map(
        functools.partial(shards, heads, ctxs, group),
        mesh=mesh,
        in_specs=(
            P("ctx", "head"),
            P("ctx", "head"),
            P("ctx", "head"),
            P(("head", "ctx"), None),
            P(("head", "ctx")),
            P(("head", "ctx"), None),
        ),
        out_specs=(P("ctx", "head"), P("ctx", "head"), P("ctx", "head")),
        check_vma=False,
    )
```

```python
import functools
import math

import jax
import jax.numpy as jnp
from jax import lax
from jax.experimental import pallas as pl
from jax.experimental.pallas import tpu as pltpu
from jax.sharding import PartitionSpec as P

DH = 128
CAP = 3
GROUP = 8
CHUNK = 512
MASKED = -1e30
MESH = pl.DeviceIdType.MESH
F32 = jnp.float32
BF16 = jnp.bfloat16


def dot_nt(a, b):
    return lax.dot_general(a, b, (((1,), (1,)), ((), ())), preferred_element_type=F32)


def dot_nn(a, b):
    return lax.dot_general(a, b, (((1,), (0,)), ((), ())), preferred_element_type=F32)


def iota(shape, dim):
    return lax.broadcasted_iota(jnp.int32, shape, dim)


def kernel(heads, ctxs, group, *refs):
    (q_hbm, k_hbm, v_hbm, t_hbm, slots_hbm, spans_hbm, out_ref) = refs[:7]
    (slots_in, spans_in, hop1_in, hop2_out, hop2_in) = refs[7:12]
    (qg, dog, kb, vb, kt, pt, p16, dp, mrow, lse_st, del_st, drow) = refs[12:24]
    (dqa, dq_out, dq_in, dk_out, dk_in, dk_own, dv_out, dv_in, dv_own) = refs[24:33]
    (dk_part, dk_land, dk_keep, dv_part, dv_land, dv_keep) = refs[33:39]
    (in_sem, h_send, h_recv, c_send, c_recv, q_send, q_recv, do_send, do_recv) = refs[39:48]
    (l_send, l_recv, d_send, d_recv, dq_send, dq_recv) = refs[48:54]
    (k_send, k_recv, v_send, v_recv, kn_send, kn_recv, vn_send, vn_recv) = refs[54:62]
    (pv_send, pv_recv, pk_send, pk_recv, dk_send, dk_recv, dv_send, dv_recv) = refs[62:]
    me_h = lax.axis_index("head")
    me_c = lax.axis_index("ctx")
    z = lax.div(me_c, group)
    r = lax.rem(me_c, group)
    base = z * group
    core = lax.rem(r, 2)
    chip = lax.div(r, 2)
    chips = group // 2
    sibling = r + 1 - 2 * core
    rows = q_hbm.shape[0]
    trows = t_hbm.shape[0]
    lines = ctxs // group
    chunks = chips * rows // CHUNK
    per_chunk = CHUNK // rows
    other = 1 - core
    scale = 1.0 / math.sqrt(DH)

    def each(start, stop, f):
        def body(i, carry):
            f(i)
            return carry

        lax.fori_loop(start, stop, body, 0)

    def every(start, stop, f):
        for i in range(start, stop):
            f(i)

    def mate(i):
        return lax.rem(chip + i, chips)

    def device(of_chip):
        return (me_h, base + 2 * of_chip + core)

    def block(index):
        return pl.ds(pl.multiple_of(index * rows, rows), rows)

    def remote(src, dst, send, recv, device):
        return pltpu.make_async_remote_copy(
            src_ref=src,
            dst_ref=dst,
            send_sem=send,
            recv_sem=recv,
            device_id=device,
            device_id_type=MESH,
        )

    def hop1(i):
        peer = lax.rem(me_h + i, heads)
        columns = pl.ds(pl.multiple_of(peer * DH, DH), DH)
        return [
            remote(src, dst, h_send, sem, (peer, me_c))
            for src, dst, sem in (
                (slots_hbm, slots_in.at[me_h], h_recv.at[0]),
                (spans_hbm, spans_in.at[me_h], h_recv.at[1]),
                (t_hbm.at[:, columns], hop1_in.at[me_h, pl.ds(0, trows), :], h_recv.at[2]),
            )
        ]

    def hop1_all():
        most = pl.ds(0, heads - 1)
        here = (
            slots_in.at[most],
            spans_in.at[most],
            hop1_in.at[most, pl.ds(0, trows), :],
        )
        return [
            remote(ref, ref, h_send, h_recv.at[j], (me_h, me_c)) for j, ref in enumerate(here)
        ]

    def hop2(i):
        peer = lax.rem(me_c + i, ctxs)
        return remote(hop2_out.at[peer], hop2_in.at[me_c], c_send, c_recv, (me_h, peer))

    def hop2_all():
        most = pl.ds(0, ctxs - 1)
        return remote(hop2_out.at[most], hop2_in.at[most], c_send, c_recv, (me_h, me_c))

    def share_start(buffer, send, recv):
        here = buffer.at[block(chip), :]
        every(1, chips, lambda i: remote(here, here, send, recv, device(mate(i))).start())

    def share_all(buffer, send, recv):
        most = buffer.at[pl.ds(0, (chips - 1) * rows), :]
        return remote(most, most, send, recv, (me_h, me_c))

    def to_line(buffer, send, recv, line):
        here = buffer.at[z, core]
        return remote(here, here, send.at[line], recv.at[z], (me_h, line * group + r))

    def from_line(buffer, send, recv, line):
        here = buffer.at[line, core]
        return remote(here, here, send.at[line], recv.at[line], (me_h, line * group + r))

    def near(buffer, send, recv, line):
        here = buffer.at[line, core]
        return remote(here, here, send.at[line], recv.at[line], (me_h, base + sibling))

    def near_arrival(buffer, send, recv, line):
        here = buffer.at[line, other]
        return remote(here, here, send.at[line], recv.at[line], (me_h, base + sibling))

    def forward(buffer, send, recv, near_send, near_recv):
        def step(line):
            from_line(buffer, send, recv, line).wait_recv()
            near(buffer, near_send, near_recv, line).start()

        each(0, z, step)

    def part(out, landing, send, recv, line):
        return remote(
            out.at[line], landing.at[line], send.at[line], recv.at[line], (me_h, base + sibling)
        )

    def stat(buffer, send, recv, i):
        return remote(buffer.at[chip], buffer.at[chip], send, recv, device(mate(i)))

    def stat_all(buffer, send, recv):
        most = buffer.at[pl.ds(0, chips - 1)]
        return remote(most, most, send, recv, (me_h, me_c))

    def back(out, landing, send, recv, line):
        return remote(
            out.at[line], landing.at[z], send.at[line], recv.at[z], (me_h, line * group + r)
        )

    def back_arrival(out, landing, send, recv, line):
        return remote(
            out.at[line], landing.at[line], send.at[line], recv.at[line], (me_h, line * group + r)
        )

    def dq_away(i):
        return remote(
            dq_out.at[mate(i)], dq_in.at[chip], dq_send.at[i], dq_recv.at[chip], device(mate(i))
        )

    def dq_arrival(i):
        return remote(
            dq_out.at[mate(i)], dq_in.at[mate(i)], dq_send.at[i], dq_recv.at[mate(i)], device(mate(i))
        )

    barrier = pltpu.get_barrier_semaphore()

    def greet(device):
        pl.semaphore_signal(barrier, inc=1, device_id=device, device_id_type=MESH)

    loads = [
        pltpu.make_async_copy(q_hbm, qg.at[block(chip), :], in_sem.at[0]),
        pltpu.make_async_copy(k_hbm, kb.at[z, core], in_sem.at[1]),
        pltpu.make_async_copy(v_hbm, vb.at[z, core], in_sem.at[2]),
        pltpu.make_async_copy(slots_hbm, slots_in.at[me_h], in_sem.at[3]),
        pltpu.make_async_copy(spans_hbm, spans_in.at[me_h], in_sem.at[4]),
        pltpu.make_async_copy(
            t_hbm.at[:, pl.ds(pl.multiple_of(me_h * DH, DH), DH)],
            hop1_in.at[me_h, pl.ds(0, trows), :],
            in_sem.at[5],
        ),
    ]
    every(1, heads, lambda i: greet((lax.rem(me_h + i, heads), me_c)))
    every(1, ctxs, lambda i: greet((me_h, lax.rem(me_c + i, ctxs))))
    for load in loads:
        load.start()
    hop1_in[:, trows:64, :] = jnp.zeros((heads, 64 - trows, DH), BF16)

    pl.semaphore_wait(barrier, heads - 1 + ctxs - 1)

    def hop1_start(i):
        for copy in hop1(i):
            copy.start()

    every(1, heads, hop1_start)
    for load in loads:
        load.wait()
    share_start(qg, q_send, q_recv)
    each(z + 1, lines, lambda line: to_line(kb, k_send, k_recv, line).start())
    near(kb, kn_send, kn_recv, z).start()
    near(vb, vn_send, vn_recv, z).start()
    for copy in hop1_all():
        copy.wait_recv()

    kdepth = heads * 64
    teacher = hop1_in[...].reshape(kdepth, DH)
    eye = iota((64, trows), 0) == iota((64, trows), 1)
    ones = jnp.ones((trows, DH), BF16)
    firsts, lasts = [], []
    slots = jnp.zeros((16, trows), F32)
    for h in range(heads):
        spans = spans_in[h].astype(F32)
        firsts.append(jnp.where(eye, spans[0:1], 0.0).astype(BF16))
        lasts.append(jnp.where(eye, spans[1:2], 0.0).astype(BF16))
        slots = jnp.where(iota((16, trows), 0) == h, slots_in[h].astype(F32), slots)
    first = dot_nn(jnp.concatenate(firsts, axis=0), ones).astype(BF16)
    last = dot_nn(jnp.concatenate(lasts, axis=0), ones).astype(BF16)
    place = jnp.bitwise_and(iota((trows, DH), 1), 63)
    pick = (place == iota((trows, DH), 0)).astype(F32).astype(BF16)
    slots = dot_nn(slots.astype(BF16), pick) + 128.0 * iota((16, DH), 0).astype(F32)
    unused = jnp.bitwise_and(iota((16, DH), 1), 63) >= trows
    slots = jnp.where(unused, -1.0, slots)
    left = iota((1, DH), 1) < 64
    codes = [
        jnp.where(left, slots[h : h + 1], slots[h + 1 : h + 2]) for h in range(0, heads, 2)
    ]
    mine = lax.rem(me_c, 4) * 32

    def pack(step):
        row = iota((256, DH), 0)
        within = jnp.bitwise_and(row, 31)
        dest = lax.shift_right_logical(row, 5) + step * 8
        spot = lax.div(within, heads)
        head = within - spot * heads
        wanted = jnp.where(spot < CAP, dest * CAP + spot + 128 * head, -5).astype(F32)
        chosen = [(wanted == code).astype(F32).astype(BF16) for code in codes]
        chosen = jnp.concatenate(chosen, axis=1)
        moved = dot_nn(chosen, teacher).reshape(8, 32, DH)
        diagonal = (iota((256, DH), 1) == within + mine).astype(F32)
        lower = (dot_nn(chosen, first) * diagonal).reshape(8, 32, DH)
        upper = (dot_nn(chosen, last) * diagonal).reshape(8, 32, DH)
        lower = jnp.sum(lower, axis=1, keepdims=True)
        upper = jnp.sum(upper, axis=1, keepdims=True)
        line = iota((8, 8, DH), 1)
        tail = jnp.where(line == 0, lower, jnp.where(line == 1, upper, 0.0))
        message = jnp.concatenate([moved[:, 0:24, :], tail], axis=1)
        hop2_out[pl.ds(step * 8, 8)] = message.astype(BF16)

    for step in range(ctxs // 8):
        pack(step)
    for i in sorted(range(1, ctxs), key=lambda i: min(i, ctxs - i)):
        hop2(i).start()
    hop2_in[me_c] = hop2_out[me_c]

    each(z + 1, lines, lambda line: to_line(vb, v_send, v_recv, line).start())
    forward(kb, k_send, k_recv, kn_send, kn_recv)
    share_all(qg, q_send, q_recv).wait_recv()

    def transpose_keys(line):
        near_arrival(kb, kn_send, kn_recv, line).wait_recv()
        for side in range(2):
            kt[line, side] = kb[line, side].astype(F32).T.astype(BF16)

    each(0, z + 1, transpose_keys)

    def scores_chunk(qc):
        queries = qg[pl.ds(pl.multiple_of(qc * CHUNK, CHUNK), CHUNK), :]

        def score(line, top):
            for side in range(2):
                s = dot_nt(kb[line, side], queries)
                pt[line, side, qc] = s
                top = jnp.maximum(top, jnp.max(s, axis=0, keepdims=True))
            return top

        top = lax.fori_loop(0, z, score, jnp.full((1, CHUNK), MASKED, F32))
        place = iota((rows, CHUNK), 1) + qc * CHUNK
        query_pos = place + (lax.div(place, rows) + core) * rows
        for side in range(2):
            s = dot_nt(kb[z, side], queries)
            key_pos = iota((rows, CHUNK), 0) + (2 * chip + side) * rows
            s = jnp.where(key_pos <= query_pos, s, MASKED)
            pt[z, side, qc] = s
            top = jnp.maximum(top, jnp.max(s, axis=0, keepdims=True))

        def weight(line, total):
            for side in range(2):
                p = jnp.exp((pt[line, side, qc] - top) * scale)
                pt[line, side, qc] = p
                total = total + jnp.sum(p, axis=0, keepdims=True)
            return total

        total = lax.fori_loop(0, z + 1, weight, jnp.zeros((1, CHUNK), F32))
        mrow[qc] = top * scale
        lse_st[chip, qc] = top * scale + jnp.log(total)

    each(0, chunks, scores_chunk)
    every(1, chips, lambda i: stat(lse_st, l_send, l_recv, i).start())
    stat_all(lse_st, l_send, l_recv).wait_recv()

    def probs_chunk(qc):
        parts = lse_st[:, qc]
        top = jnp.max(parts, axis=0)
        lse = top + jnp.log(jnp.sum(jnp.exp(parts - top[None]), axis=0))
        fade = jnp.exp(mrow[qc] - lse)

        def fix(line):
            for side in range(2):
                prob = pt[line, side, qc] * fade
                pt[line, side, qc] = prob
                p16[line, side, qc] = prob.astype(BF16)

        each(0, z + 1, fix)

    each(0, chunks, probs_chunk)

    hop2_all().wait_recv()
    token = iota((rows, DH), 0).astype(F32)

    def cover(step, total):
        four = hop2_in[pl.ds(step * 4, 4)]
        edges = jnp.sum(four[:, 16:32, :].astype(F32), axis=0)
        lower = edges[8:9]
        upper = edges[9:10]
        covered = jnp.where((token >= lower) & (token < upper), 1.0, 0.0).astype(BF16)
        return total + dot_nn(covered, four.reshape(4 * 32, DH))

    grad = jnp.zeros((rows, DH), F32)
    for step in range(ctxs // 4):
        grad = cover(step, grad)
    dog[block(chip), :] = grad.astype(BF16)
    share_start(dog, do_send, do_recv)

    forward(vb, v_send, v_recv, vn_send, vn_recv)
    share_all(dog, do_send, do_recv).wait_recv()

    def value_terms(line, side):
        total = jnp.zeros((rows, DH), F32)
        for qc in range(chunks):
            total += dot_nn(p16[line, side, qc], dog[qc * CHUNK : (qc + 1) * CHUNK, :])
        return total

    def value_join(line):
        part(dv_part, dv_land, pv_send, pv_recv, line).wait_recv()
        dv_out[line] = (dv_keep[line] + dv_land[line].astype(F32)).astype(BF16)
        back(dv_out, dv_in, dv_send, dv_recv, line).start()

    def value_parts(line):
        dv_part[line] = value_terms(line, other).astype(BF16)
        part(dv_part, dv_land, pv_send, pv_recv, line).start()
        dv_keep[line] = value_terms(line, core)
        pl.when(line > 0)(lambda: value_join(line - 1))

    each(0, z + 1, value_parts)

    def grad_probs(line, sums):
        for side in range(2):
            for qc in range(chunks):
                d = dot_nt(vb[line, side], dog[qc * CHUNK : (qc + 1) * CHUNK, :])
                dp[line, side, qc] = d
                here = jnp.sum(pt[line, side, qc] * d, axis=0, keepdims=True)
                sums[qc] = here if sums[qc] is None else sums[qc] + here
        return sums

    near_arrival(vb, vn_send, vn_recv, z).wait_recv()
    sums = grad_probs(z, [None] * chunks)
    for qc in range(chunks):
        del_st[chip, qc] = sums[qc]

    def earlier_probs(i):
        line = z - i
        near_arrival(vb, vn_send, vn_recv, line).wait_recv()
        sums = grad_probs(line, [None] * chunks)
        for qc in range(chunks):
            del_st[chip, qc] += sums[qc]

    each(1, z + 1, earlier_probs)
    every(1, chips, lambda i: stat(del_st, d_send, d_recv, i).start())

    for copy in hop1_all():
        copy.wait_send()
    hop2_all().wait_send()
    share_all(qg, q_send, q_recv).wait_send()
    share_all(dog, do_send, do_recv).wait_send()
    stat_all(lse_st, l_send, l_recv).wait_send()

    def lines_sent(line):
        to_line(kb, k_send, k_recv, line).wait_send()
        to_line(vb, v_send, v_recv, line).wait_send()

    each(z + 1, lines, lines_sent)

    def nears_sent(line):
        near(kb, kn_send, kn_recv, line).wait_send()
        near(vb, vn_send, vn_recv, line).wait_send()
        part(dv_part, dv_land, pv_send, pv_recv, line).wait_send()

    each(0, z + 1, nears_sent)
    for j in range(chips):
        dqa[j] = jnp.zeros((DH, rows), F32)

    stat_all(del_st, d_send, d_recv).wait_recv()
    stat_all(del_st, d_send, d_recv).wait_send()

    def deltas(qc):
        drow[qc] = jnp.sum(del_st[:, qc], axis=0)

    each(0, chunks, deltas)

    def dscores(line, side):
        for qc in range(chunks):
            dscore = (pt[line, side, qc] * (dp[line, side, qc] - drow[qc]) * scale).astype(BF16)
            p16[line, side, qc] = dscore

    def query_terms(line):
        for qc in range(chunks):
            terms = dot_nn(kt[line, 0], p16[line, 0, qc]) + dot_nn(kt[line, 1], p16[line, 1, qc])
            for j in range(per_chunk):
                dqa[qc * per_chunk + j] += terms[:, j * rows : (j + 1) * rows]

    def key_terms(line, side):
        total = jnp.zeros((rows, DH), F32)
        for qc in range(chunks):
            total += dot_nn(p16[line, side, qc], qg[qc * CHUNK : (qc + 1) * CHUNK, :])
        return total

    def key_parts(line):
        dk_part[line] = key_terms(line, other).astype(BF16)
        part(dk_part, dk_land, pk_send, pk_recv, line).start()

    def key_keeps(line):
        dk_keep[line] = key_terms(line, core)

    def key_sum(line):
        part(dk_part, dk_land, pk_send, pk_recv, line).wait_recv()
        return dk_keep[line] + dk_land[line].astype(F32)

    def key_join(line):
        dk_out[line] = key_sum(line).astype(BF16)
        back(dk_out, dk_in, dk_send, dk_recv, line).start()

    def earlier_keys(line):
        dscores(line, other)
        key_parts(line)
        dscores(line, core)
        key_keeps(line)
        pl.when(line > 0)(lambda: key_join(line - 1))

    each(0, z, earlier_keys)
    dscores(z, other)
    dscores(z, core)
    pl.when(z > 0)(lambda: key_join(z - 1))
    each(0, z + 1, query_terms)
    dq_out[...] = dqa[...].astype(BF16)
    every(1, chips, lambda i: dq_away(i).start())
    key_parts(z)
    key_keeps(z)

    part(dv_part, dv_land, pv_send, pv_recv, z).wait_recv()
    dv_own[...] = dv_keep[z] + dv_land[z].astype(F32)

    def dv_add(line):
        back_arrival(dv_out, dv_in, dv_send, dv_recv, line).wait_recv()
        dv_own[...] += dv_in[line].astype(F32)

    each(z + 1, lines, dv_add)
    out_ref[2] = dv_own[...].astype(BF16)
    dk_own[...] = key_sum(z)

    def dk_add(line):
        back_arrival(dk_out, dk_in, dk_send, dk_recv, line).wait_recv()
        dk_own[...] += dk_in[line].astype(F32)

    each(z + 1, lines, dk_add)
    out_ref[1] = dk_own[...].astype(BF16)

    def dq_add(i, total):
        dq_arrival(i).wait_recv()
        return total + dq_in[mate(i)].astype(F32)

    dq_total = lax.fori_loop(1, chips, dq_add, dqa[chip])
    out_ref[0] = dq_total.T.astype(BF16)

    every(1, chips, lambda i: dq_away(i).wait_send())
    each(0, z + 1, lambda line: part(dk_part, dk_land, pk_send, pk_recv, line).wait_send())

    def backs_sent(line):
        back(dv_out, dv_in, dv_send, dv_recv, line).wait_send()
        back(dk_out, dk_in, dk_send, dk_recv, line).wait_send()

    each(0, z, backs_sent)


def shards(heads, ctxs, group, queries, keys, values, teacher_rows, slots, spans):
    rows = queries.shape[0]
    trows = teacher_rows.shape[0]
    lines = ctxs // group
    chips = group // 2
    chunks = chips * rows // CHUNK
    vm = pltpu.VMEM
    dma = pltpu.SemaphoreType.DMA
    parts = [vm((lines, rows, DH), BF16), vm((lines, rows, DH), BF16)]
    scratch = [
        vm((heads, 1, trows), jnp.int32),
        vm((heads, 2, trows), jnp.int32),
        vm((heads, 64, DH), BF16),
        vm((ctxs, 32, DH), BF16),
        vm((ctxs, 32, DH), BF16),
        vm((chips * rows, DH), BF16),
        vm((chips * rows, DH), BF16),
        vm((lines, 2, rows, DH), BF16),
        vm((lines, 2, rows, DH), BF16),
        vm((lines, 2, DH, rows), BF16),
        vm((lines, 2, chunks, rows, CHUNK), F32),
        vm((lines, 2, chunks, rows, CHUNK), BF16),
        vm((lines, 2, chunks, rows, CHUNK), F32),
        vm((chunks, 1, CHUNK), F32),
        vm((chips, chunks, 1, CHUNK), F32),
        vm((chips, chunks, 1, CHUNK), F32),
        vm((chunks, 1, CHUNK), F32),
        vm((chips, DH, rows), F32),
        vm((chips, DH, rows), BF16),
        vm((chips, DH, rows), BF16),
        *parts,
        vm((rows, DH), F32),
        *parts,
        vm((rows, DH), F32),
        *parts,
        vm((lines, rows, DH), F32),
        *parts,
        vm((lines, rows, DH), F32),
        dma((6,)),
        dma,
        dma((3,)),
        *([dma] * 10),
        dma((chips,)),
        dma((chips,)),
        *([dma((lines,))] * 16),
    ]
    out = pl.pallas_call(
        functools.partial(kernel, heads, ctxs, group),
        out_shape=pltpu.VMEM((3, rows, DH), BF16),
        in_specs=[pl.BlockSpec(memory_space=pl.ANY)] * 6,
        out_specs=pl.BlockSpec(memory_space=pltpu.VMEM),
        scratch_shapes=scratch,
        compiler_params=pltpu.CompilerParams(
            collective_id=0, has_side_effects=True, vmem_limit_bytes=56 * 1024 * 1024
        ),
        name="attention_backward",
    )(queries, keys, values, teacher_rows, slots.reshape(1, trows), spans.T)
    return out[0], out[1], out[2]


def solution(mesh):
    heads, ctxs = mesh.shape["head"], mesh.shape["ctx"]
    group = min(GROUP, ctxs // 2)
    return jax.shard_map(
        functools.partial(shards, heads, ctxs, group),
        mesh=mesh,
        in_specs=(
            P("ctx", "head"),
            P("ctx", "head"),
            P("ctx", "head"),
            P(("head", "ctx"), None),
            P(("head", "ctx")),
            P(("head", "ctx"), None),
        ),
        out_specs=(P("ctx", "head"), P("ctx", "head"), P("ctx", "head")),
        check_vma=False,
    )
```

```python
import functools
import math

import jax
import jax.numpy as jnp
from jax import lax
from jax.experimental import pallas as pl
from jax.experimental.pallas import tpu as pltpu
from jax.sharding import PartitionSpec as P

DH = 128
CAP = 3
GROUP = 8
CHUNK = 512
MASKED = -1e30
MESH = pl.DeviceIdType.MESH
F32 = jnp.float32
BF16 = jnp.bfloat16


def dot_nt(a, b):
    return lax.dot_general(a, b, (((1,), (1,)), ((), ())), preferred_element_type=F32)


def dot_nn(a, b):
    return lax.dot_general(a, b, (((1,), (0,)), ((), ())), preferred_element_type=F32)


def iota(shape, dim):
    return lax.broadcasted_iota(jnp.int32, shape, dim)


def kernel(heads, ctxs, group, *refs):
    (q_hbm, k_hbm, v_hbm, t_hbm, slots_hbm, spans_hbm, out_ref) = refs[:7]
    (slots_in, spans_in, hop1_in, hop2_out, hop2_in) = refs[7:12]
    (qg, dog, kb, vb, kt, pt, p16, dp, mrow, lse_st, del_st, drow) = refs[12:24]
    (dqa, dq_out, dq_in, dk_out, dk_in, dk_own, dv_out, dv_in, dv_own) = refs[24:33]
    (dk_part, dk_land, dk_keep, dv_part, dv_land, dv_keep) = refs[33:39]
    (in_sem, h_send, h_recv, c_send, c_recv, q_send, q_recv, do_send, do_recv) = refs[39:48]
    (l_send, l_recv, d_send, d_recv, dq_send, dq_recv) = refs[48:54]
    (k_send, k_recv, v_send, v_recv, kn_send, kn_recv, vn_send, vn_recv) = refs[54:62]
    (pv_send, pv_recv, pk_send, pk_recv, dk_send, dk_recv, dv_send, dv_recv) = refs[62:]
    me_h = lax.axis_index("head")
    me_c = lax.axis_index("ctx")
    z = lax.div(me_c, group)
    r = lax.rem(me_c, group)
    base = z * group
    core = lax.rem(r, 2)
    chip = lax.div(r, 2)
    chips = group // 2
    sibling = r + 1 - 2 * core
    rows = q_hbm.shape[0]
    trows = t_hbm.shape[0]
    lines = ctxs // group
    chunks = chips * rows // CHUNK
    per_chunk = CHUNK // rows
    other = 1 - core
    scale = 1.0 / math.sqrt(DH)

    def each(start, stop, f):
        def body(i, carry):
            f(i)
            return carry

        lax.fori_loop(start, stop, body, 0)

    def every(start, stop, f):
        for i in range(start, stop):
            f(i)

    def mate(i):
        return lax.rem(chip + i, chips)

    def device(of_chip):
        return (me_h, base + 2 * of_chip + core)

    def block(index):
        return pl.ds(pl.multiple_of(index * rows, rows), rows)

    def remote(src, dst, send, recv, device):
        return pltpu.make_async_remote_copy(
            src_ref=src,
            dst_ref=dst,
            send_sem=send,
            recv_sem=recv,
            device_id=device,
            device_id_type=MESH,
        )

    def hop1(i):
        peer = lax.rem(me_h + i, heads)
        columns = pl.ds(pl.multiple_of(peer * DH, DH), DH)
        return [
            remote(src, dst, h_send, sem, (peer, me_c))
            for src, dst, sem in (
                (slots_hbm, slots_in.at[me_h], h_recv.at[0]),
                (spans_hbm, spans_in.at[me_h], h_recv.at[1]),
                (t_hbm.at[:, columns], hop1_in.at[me_h, pl.ds(0, trows), :], h_recv.at[2]),
            )
        ]

    def hop1_all():
        most = pl.ds(0, heads - 1)
        here = (
            slots_in.at[most],
            spans_in.at[most],
            hop1_in.at[most, pl.ds(0, trows), :],
        )
        return [
            remote(ref, ref, h_send, h_recv.at[j], (me_h, me_c)) for j, ref in enumerate(here)
        ]

    def hop2(i):
        peer = lax.rem(me_c + i, ctxs)
        return remote(hop2_out.at[peer], hop2_in.at[me_c], c_send, c_recv, (me_h, peer))

    def hop2_all():
        most = pl.ds(0, ctxs - 1)
        return remote(hop2_out.at[most], hop2_in.at[most], c_send, c_recv, (me_h, me_c))

    def share_start(buffer, send, recv):
        here = buffer.at[block(chip), :]
        every(1, chips, lambda i: remote(here, here, send, recv, device(mate(i))).start())

    def share_all(buffer, send, recv):
        most = buffer.at[pl.ds(0, (chips - 1) * rows), :]
        return remote(most, most, send, recv, (me_h, me_c))

    def to_line(buffer, send, recv, line):
        here = buffer.at[z, core]
        return remote(here, here, send.at[line], recv.at[z], (me_h, line * group + r))

    def from_line(buffer, send, recv, line):
        here = buffer.at[line, core]
        return remote(here, here, send.at[line], recv.at[line], (me_h, line * group + r))

    def near(buffer, send, recv, line):
        here = buffer.at[line, core]
        return remote(here, here, send.at[line], recv.at[line], (me_h, base + sibling))

    def near_arrival(buffer, send, recv, line):
        here = buffer.at[line, other]
        return remote(here, here, send.at[line], recv.at[line], (me_h, base + sibling))

    def forward(buffer, send, recv, near_send, near_recv):
        def step(line):
            from_line(buffer, send, recv, line).wait_recv()
            near(buffer, near_send, near_recv, line).start()

        each(0, z, step)

    def part(out, landing, send, recv, line):
        return remote(
            out.at[line], landing.at[line], send.at[line], recv.at[line], (me_h, base + sibling)
        )

    def stat(buffer, send, recv, i):
        return remote(buffer.at[chip], buffer.at[chip], send, recv, device(mate(i)))

    def stat_all(buffer, send, recv):
        most = buffer.at[pl.ds(0, chips - 1)]
        return remote(most, most, send, recv, (me_h, me_c))

    def back(out, landing, send, recv, line):
        return remote(
            out.at[line], landing.at[z], send.at[line], recv.at[z], (me_h, line * group + r)
        )

    def back_arrival(out, landing, send, recv, line):
        return remote(
            out.at[line], landing.at[line], send.at[line], recv.at[line], (me_h, line * group + r)
        )

    def dq_away(i):
        return remote(
            dq_out.at[mate(i)], dq_in.at[chip], dq_send.at[i], dq_recv.at[chip], device(mate(i))
        )

    def dq_arrival(i):
        return remote(
            dq_out.at[mate(i)], dq_in.at[mate(i)], dq_send.at[i], dq_recv.at[mate(i)], device(mate(i))
        )

    barrier = pltpu.get_barrier_semaphore()

    def greet(device):
        pl.semaphore_signal(barrier, inc=1, device_id=device, device_id_type=MESH)

    loads = [
        pltpu.make_async_copy(q_hbm, qg.at[block(chip), :], in_sem.at[0]),
        pltpu.make_async_copy(k_hbm, kb.at[z, core], in_sem.at[1]),
        pltpu.make_async_copy(v_hbm, vb.at[z, core], in_sem.at[2]),
        pltpu.make_async_copy(slots_hbm, slots_in.at[me_h], in_sem.at[3]),
        pltpu.make_async_copy(spans_hbm, spans_in.at[me_h], in_sem.at[4]),
        pltpu.make_async_copy(
            t_hbm.at[:, pl.ds(pl.multiple_of(me_h * DH, DH), DH)],
            hop1_in.at[me_h, pl.ds(0, trows), :],
            in_sem.at[5],
        ),
    ]
    every(1, heads, lambda i: greet((lax.rem(me_h + i, heads), me_c)))
    every(1, ctxs, lambda i: greet((me_h, lax.rem(me_c + i, ctxs))))
    for load in loads:
        load.start()
    hop1_in[:, trows:64, :] = jnp.zeros((heads, 64 - trows, DH), BF16)

    pl.semaphore_wait(barrier, heads - 1 + ctxs - 1)

    def hop1_start(i):
        for copy in hop1(i):
            copy.start()

    every(1, heads, hop1_start)
    for load in loads:
        load.wait()
    share_start(qg, q_send, q_recv)
    each(z + 1, lines, lambda line: to_line(kb, k_send, k_recv, line).start())
    near(kb, kn_send, kn_recv, z).start()
    near(vb, vn_send, vn_recv, z).start()
    for copy in hop1_all():
        copy.wait_recv()

    kdepth = heads * 64
    teacher = hop1_in[...].reshape(kdepth, DH)
    eye = iota((64, trows), 0) == iota((64, trows), 1)
    ones = jnp.ones((trows, DH), BF16)
    firsts, lasts = [], []
    slots = jnp.zeros((16, trows), F32)
    for h in range(heads):
        spans = spans_in[h].astype(F32)
        firsts.append(jnp.where(eye, spans[0:1], 0.0).astype(BF16))
        lasts.append(jnp.where(eye, spans[1:2], 0.0).astype(BF16))
        slots = jnp.where(iota((16, trows), 0) == h, slots_in[h].astype(F32), slots)
    first = dot_nn(jnp.concatenate(firsts, axis=0), ones).astype(BF16)
    last = dot_nn(jnp.concatenate(lasts, axis=0), ones).astype(BF16)
    place = jnp.bitwise_and(iota((trows, DH), 1), 63)
    pick = (place == iota((trows, DH), 0)).astype(F32).astype(BF16)
    slots = dot_nn(slots.astype(BF16), pick) + 128.0 * iota((16, DH), 0).astype(F32)
    unused = jnp.bitwise_and(iota((16, DH), 1), 63) >= trows
    slots = jnp.where(unused, -1.0, slots)
    left = iota((1, DH), 1) < 64
    codes = [
        jnp.where(left, slots[h : h + 1], slots[h + 1 : h + 2]) for h in range(0, heads, 2)
    ]
    mine = lax.rem(me_c, 4) * 32

    def pack(step):
        row = iota((256, DH), 0)
        within = jnp.bitwise_and(row, 31)
        dest = lax.shift_right_logical(row, 5) + step * 8
        spot = lax.div(within, heads)
        head = within - spot * heads
        wanted = jnp.where(spot < CAP, dest * CAP + spot + 128 * head, -5).astype(F32)
        chosen = [(wanted == code).astype(F32).astype(BF16) for code in codes]
        chosen = jnp.concatenate(chosen, axis=1)
        moved = dot_nn(chosen, teacher).reshape(8, 32, DH)
        diagonal = (iota((256, DH), 1) == within + mine).astype(F32)
        lower = (dot_nn(chosen, first) * diagonal).reshape(8, 32, DH)
        upper = (dot_nn(chosen, last) * diagonal).reshape(8, 32, DH)
        lower = jnp.sum(lower, axis=1, keepdims=True)
        upper = jnp.sum(upper, axis=1, keepdims=True)
        line = iota((8, 8, DH), 1)
        tail = jnp.where(line == 0, lower, jnp.where(line == 1, upper, 0.0))
        message = jnp.concatenate([moved[:, 0:24, :], tail], axis=1)
        hop2_out[pl.ds(step * 8, 8)] = message.astype(BF16)

    for step in range(ctxs // 8):
        pack(step)
    for i in sorted(range(1, ctxs), key=lambda i: min(i, ctxs - i)):
        hop2(i).start()
    hop2_in[me_c] = hop2_out[me_c]

    each(z + 1, lines, lambda line: to_line(vb, v_send, v_recv, line).start())
    forward(kb, k_send, k_recv, kn_send, kn_recv)
    share_all(qg, q_send, q_recv).wait_recv()

    def transpose_keys(line):
        near_arrival(kb, kn_send, kn_recv, line).wait_recv()
        for side in range(2):
            kt[line, side] = kb[line, side].astype(F32).T.astype(BF16)

    each(0, z + 1, transpose_keys)

    def scores_chunk(qc):
        queries = qg[pl.ds(pl.multiple_of(qc * CHUNK, CHUNK), CHUNK), :]

        def score(line, top):
            for side in range(2):
                s = dot_nt(kb[line, side], queries)
                pt[line, side, qc] = s
                top = jnp.maximum(top, jnp.max(s, axis=0, keepdims=True))
            return top

        top = lax.fori_loop(0, z, score, jnp.full((1, CHUNK), MASKED, F32))
        place = iota((rows, CHUNK), 1) + qc * CHUNK
        query_pos = place + (lax.div(place, rows) + core) * rows
        for side in range(2):
            s = dot_nt(kb[z, side], queries)
            key_pos = iota((rows, CHUNK), 0) + (2 * chip + side) * rows
            s = jnp.where(key_pos <= query_pos, s, MASKED)
            pt[z, side, qc] = s
            top = jnp.maximum(top, jnp.max(s, axis=0, keepdims=True))

        def weight(line, total):
            for side in range(2):
                p = jnp.exp((pt[line, side, qc] - top) * scale)
                pt[line, side, qc] = p
                total = total + jnp.sum(p, axis=0, keepdims=True)
            return total

        total = lax.fori_loop(0, z + 1, weight, jnp.zeros((1, CHUNK), F32))
        mrow[qc] = top * scale
        lse_st[chip, qc] = top * scale + jnp.log(total)

    each(0, chunks, scores_chunk)
    every(1, chips, lambda i: stat(lse_st, l_send, l_recv, i).start())
    stat_all(lse_st, l_send, l_recv).wait_recv()

    def probs_chunk(qc):
        parts = lse_st[:, qc]
        top = jnp.max(parts, axis=0)
        lse = top + jnp.log(jnp.sum(jnp.exp(parts - top[None]), axis=0))
        fade = jnp.exp(mrow[qc] - lse)

        def fix(line):
            for side in range(2):
                prob = pt[line, side, qc] * fade
                pt[line, side, qc] = prob
                p16[line, side, qc] = prob.astype(BF16)

        each(0, z + 1, fix)

    each(0, chunks, probs_chunk)

    hop2_all().wait_recv()
    token = iota((rows, DH), 0).astype(F32)

    def cover(step, total):
        four = hop2_in[pl.ds(step * 4, 4)]
        edges = jnp.sum(four[:, 16:32, :].astype(F32), axis=0)
        lower = edges[8:9]
        upper = edges[9:10]
        covered = jnp.where((token >= lower) & (token < upper), 1.0, 0.0).astype(BF16)
        return total + dot_nn(covered, four.reshape(4 * 32, DH))

    grad = jnp.zeros((rows, DH), F32)
    for step in range(ctxs // 4):
        grad = cover(step, grad)
    dog[block(chip), :] = grad.astype(BF16)
    share_start(dog, do_send, do_recv)

    forward(vb, v_send, v_recv, vn_send, vn_recv)
    share_all(dog, do_send, do_recv).wait_recv()

    def grad_probs(line, sums):
        for side in range(2):
            for qc in range(chunks):
                d = dot_nt(vb[line, side], dog[qc * CHUNK : (qc + 1) * CHUNK, :])
                dp[line, side, qc] = d
                here = jnp.sum(pt[line, side, qc] * d, axis=0, keepdims=True)
                sums[qc] = here if sums[qc] is None else sums[qc] + here
        return sums

    near_arrival(vb, vn_send, vn_recv, z).wait_recv()
    sums = grad_probs(z, [None] * chunks)
    for qc in range(chunks):
        del_st[chip, qc] = sums[qc]

    def earlier_probs(i):
        line = z - i
        near_arrival(vb, vn_send, vn_recv, line).wait_recv()
        sums = grad_probs(line, [None] * chunks)
        for qc in range(chunks):
            del_st[chip, qc] += sums[qc]

    each(1, z + 1, earlier_probs)
    every(1, chips, lambda i: stat(del_st, d_send, d_recv, i).start())

    def value_terms(line, side):
        total = jnp.zeros((rows, DH), F32)
        for qc in range(chunks):
            total += dot_nn(p16[line, side, qc], dog[qc * CHUNK : (qc + 1) * CHUNK, :])
        return total

    def value_join(line):
        part(dv_part, dv_land, pv_send, pv_recv, line).wait_recv()
        dv_out[line] = (dv_keep[line] + dv_land[line].astype(F32)).astype(BF16)
        back(dv_out, dv_in, dv_send, dv_recv, line).start()

    def value_parts(line):
        dv_part[line] = value_terms(line, other).astype(BF16)
        part(dv_part, dv_land, pv_send, pv_recv, line).start()
        dv_keep[line] = value_terms(line, core)
        pl.when(line > 0)(lambda: value_join(line - 1))

    each(0, z + 1, value_parts)

    for copy in hop1_all():
        copy.wait_send()
    hop2_all().wait_send()
    share_all(qg, q_send, q_recv).wait_send()
    share_all(dog, do_send, do_recv).wait_send()
    stat_all(lse_st, l_send, l_recv).wait_send()

    def lines_sent(line):
        to_line(kb, k_send, k_recv, line).wait_send()
        to_line(vb, v_send, v_recv, line).wait_send()

    each(z + 1, lines, lines_sent)

    def nears_sent(line):
        near(kb, kn_send, kn_recv, line).wait_send()
        near(vb, vn_send, vn_recv, line).wait_send()
        part(dv_part, dv_land, pv_send, pv_recv, line).wait_send()

    each(0, z + 1, nears_sent)
    for j in range(chips):
        dqa[j] = jnp.zeros((DH, rows), F32)

    stat_all(del_st, d_send, d_recv).wait_recv()
    stat_all(del_st, d_send, d_recv).wait_send()

    def deltas(qc):
        drow[qc] = jnp.sum(del_st[:, qc], axis=0)

    each(0, chunks, deltas)

    def dscores(line, side):
        for qc in range(chunks):
            dscore = (pt[line, side, qc] * (dp[line, side, qc] - drow[qc]) * scale).astype(BF16)
            p16[line, side, qc] = dscore

    def query_terms(line):
        for qc in range(chunks):
            terms = dot_nn(kt[line, 0], p16[line, 0, qc]) + dot_nn(kt[line, 1], p16[line, 1, qc])
            for j in range(per_chunk):
                dqa[qc * per_chunk + j] += terms[:, j * rows : (j + 1) * rows]

    def key_terms(line, side):
        total = jnp.zeros((rows, DH), F32)
        for qc in range(chunks):
            total += dot_nn(p16[line, side, qc], qg[qc * CHUNK : (qc + 1) * CHUNK, :])
        return total

    def key_parts(line):
        dk_part[line] = key_terms(line, other).astype(BF16)
        part(dk_part, dk_land, pk_send, pk_recv, line).start()

    def key_keeps(line):
        dk_keep[line] = key_terms(line, core)

    def key_sum(line):
        part(dk_part, dk_land, pk_send, pk_recv, line).wait_recv()
        return dk_keep[line] + dk_land[line].astype(F32)

    def key_join(line):
        dk_out[line] = key_sum(line).astype(BF16)
        back(dk_out, dk_in, dk_send, dk_recv, line).start()

    def earlier_keys(line):
        dscores(line, other)
        key_parts(line)
        dscores(line, core)
        key_keeps(line)
        pl.when(line > 0)(lambda: key_join(line - 1))

    each(0, z, earlier_keys)
    dscores(z, other)
    dscores(z, core)
    pl.when(z > 0)(lambda: key_join(z - 1))
    each(0, z + 1, query_terms)
    dq_out[...] = dqa[...].astype(BF16)
    every(1, chips, lambda i: dq_away(i).start())
    key_parts(z)
    key_keeps(z)

    part(dv_part, dv_land, pv_send, pv_recv, z).wait_recv()
    dv_own[...] = dv_keep[z] + dv_land[z].astype(F32)

    def dv_add(line):
        back_arrival(dv_out, dv_in, dv_send, dv_recv, line).wait_recv()
        dv_own[...] += dv_in[line].astype(F32)

    each(z + 1, lines, dv_add)
    out_ref[2] = dv_own[...].astype(BF16)
    dk_own[...] = key_sum(z)

    def dk_add(line):
        back_arrival(dk_out, dk_in, dk_send, dk_recv, line).wait_recv()
        dk_own[...] += dk_in[line].astype(F32)

    each(z + 1, lines, dk_add)
    out_ref[1] = dk_own[...].astype(BF16)

    def dq_add(i, total):
        dq_arrival(i).wait_recv()
        return total + dq_in[mate(i)].astype(F32)

    dq_total = lax.fori_loop(1, chips, dq_add, dqa[chip])
    out_ref[0] = dq_total.T.astype(BF16)

    every(1, chips, lambda i: dq_away(i).wait_send())
    each(0, z + 1, lambda line: part(dk_part, dk_land, pk_send, pk_recv, line).wait_send())

    def backs_sent(line):
        back(dv_out, dv_in, dv_send, dv_recv, line).wait_send()
        back(dk_out, dk_in, dk_send, dk_recv, line).wait_send()

    each(0, z, backs_sent)


def shards(heads, ctxs, group, queries, keys, values, teacher_rows, slots, spans):
    rows = queries.shape[0]
    trows = teacher_rows.shape[0]
    lines = ctxs // group
    chips = group // 2
    chunks = chips * rows // CHUNK
    vm = pltpu.VMEM
    dma = pltpu.SemaphoreType.DMA
    parts = [vm((lines, rows, DH), BF16), vm((lines, rows, DH), BF16)]
    scratch = [
        vm((heads, 1, trows), jnp.int32),
        vm((heads, 2, trows), jnp.int32),
        vm((heads, 64, DH), BF16),
        vm((ctxs, 32, DH), BF16),
        vm((ctxs, 32, DH), BF16),
        vm((chips * rows, DH), BF16),
        vm((chips * rows, DH), BF16),
        vm((lines, 2, rows, DH), BF16),
        vm((lines, 2, rows, DH), BF16),
        vm((lines, 2, DH, rows), BF16),
        vm((lines, 2, chunks, rows, CHUNK), F32),
        vm((lines, 2, chunks, rows, CHUNK), BF16),
        vm((lines, 2, chunks, rows, CHUNK), F32),
        vm((chunks, 1, CHUNK), F32),
        vm((chips, chunks, 1, CHUNK), F32),
        vm((chips, chunks, 1, CHUNK), F32),
        vm((chunks, 1, CHUNK), F32),
        vm((chips, DH, rows), F32),
        vm((chips, DH, rows), BF16),
        vm((chips, DH, rows), BF16),
        *parts,
        vm((rows, DH), F32),
        *parts,
        vm((rows, DH), F32),
        *parts,
        vm((lines, rows, DH), F32),
        *parts,
        vm((lines, rows, DH), F32),
        dma((6,)),
        dma,
        dma((3,)),
        *([dma] * 10),
        dma((chips,)),
        dma((chips,)),
        *([dma((lines,))] * 16),
    ]
    out = pl.pallas_call(
        functools.partial(kernel, heads, ctxs, group),
        out_shape=pltpu.VMEM((3, rows, DH), BF16),
        in_specs=[pl.BlockSpec(memory_space=pl.ANY)] * 6,
        out_specs=pl.BlockSpec(memory_space=pltpu.VMEM),
        scratch_shapes=scratch,
        compiler_params=pltpu.CompilerParams(
            collective_id=0, has_side_effects=True, vmem_limit_bytes=56 * 1024 * 1024
        ),
        name="attention_backward",
    )(queries, keys, values, teacher_rows, slots.reshape(1, trows), spans.T)
    return out[0], out[1], out[2]


def solution(mesh):
    heads, ctxs = mesh.shape["head"], mesh.shape["ctx"]
    group = min(GROUP, ctxs // 2)
    return jax.shard_map(
        functools.partial(shards, heads, ctxs, group),
        mesh=mesh,
        in_specs=(
            P("ctx", "head"),
            P("ctx", "head"),
            P("ctx", "head"),
            P(("head", "ctx"), None),
            P(("head", "ctx")),
            P(("head", "ctx"), None),
        ),
        out_specs=(P("ctx", "head"), P("ctx", "head"), P("ctx", "head")),
        check_vma=False,
    )
```

```python
import functools
import math

import jax
import jax.numpy as jnp
from jax import lax
from jax.experimental import pallas as pl
from jax.experimental.pallas import tpu as pltpu
from jax.sharding import PartitionSpec as P

DH = 128
CAP = 3
GROUP = 8
CHUNK = 512
MASKED = -1e30
MESH = pl.DeviceIdType.MESH
F32 = jnp.float32
BF16 = jnp.bfloat16


def dot_nt(a, b):
    return lax.dot_general(a, b, (((1,), (1,)), ((), ())), preferred_element_type=F32)


def dot_nn(a, b):
    return lax.dot_general(a, b, (((1,), (0,)), ((), ())), preferred_element_type=F32)


def iota(shape, dim):
    return lax.broadcasted_iota(jnp.int32, shape, dim)


def kernel(heads, ctxs, group, *refs):
    (q_hbm, k_hbm, v_hbm, t_hbm, slots_hbm, spans_hbm, out_ref) = refs[:7]
    (slots_in, spans_in, hop1_in, hop2_out, hop2_in) = refs[7:12]
    (qg, dog, kb, vb, kt, pt, p16, dp, mrow, lse_st, del_st, drow) = refs[12:24]
    (dqa, dq_out, dq_in, dk_out, dk_in, dk_own, dv_out, dv_in, dv_own) = refs[24:33]
    (dk_part, dk_land, dk_keep, dv_part, dv_land, dv_keep) = refs[33:39]
    (in_sem, h_send, h_recv, c_send, c_recv, q_send, q_recv, do_send, do_recv) = refs[39:48]
    (l_send, l_recv, d_send, d_recv, dq_send, dq_recv) = refs[48:54]
    (k_send, k_recv, v_send, v_recv, kn_send, kn_recv, vn_send, vn_recv) = refs[54:62]
    (pv_send, pv_recv, pk_send, pk_recv, dk_send, dk_recv, dv_send, dv_recv) = refs[62:]
    me_h = lax.axis_index("head")
    me_c = lax.axis_index("ctx")
    z = lax.div(me_c, group)
    r = lax.rem(me_c, group)
    base = z * group
    core = lax.rem(r, 2)
    chip = lax.div(r, 2)
    chips = group // 2
    sibling = r + 1 - 2 * core
    rows = q_hbm.shape[0]
    trows = t_hbm.shape[0]
    lines = ctxs // group
    chunks = chips * rows // CHUNK
    per_chunk = CHUNK // rows
    other = 1 - core
    scale = 1.0 / math.sqrt(DH)

    def each(start, stop, f):
        def body(i, carry):
            f(i)
            return carry

        lax.fori_loop(start, stop, body, 0)

    def every(start, stop, f):
        for i in range(start, stop):
            f(i)

    def mate(i):
        return lax.rem(chip + i, chips)

    def device(of_chip):
        return (me_h, base + 2 * of_chip + core)

    def block(index):
        return pl.ds(pl.multiple_of(index * rows, rows), rows)

    def remote(src, dst, send, recv, device):
        return pltpu.make_async_remote_copy(
            src_ref=src,
            dst_ref=dst,
            send_sem=send,
            recv_sem=recv,
            device_id=device,
            device_id_type=MESH,
        )

    def hop1(i):
        peer = lax.rem(me_h + i, heads)
        columns = pl.ds(pl.multiple_of(peer * DH, DH), DH)
        return [
            remote(src, dst, h_send, sem, (peer, me_c))
            for src, dst, sem in (
                (slots_hbm, slots_in.at[me_h], h_recv.at[0]),
                (spans_hbm, spans_in.at[me_h], h_recv.at[1]),
                (t_hbm.at[:, columns], hop1_in.at[me_h, pl.ds(0, trows), :], h_recv.at[2]),
            )
        ]

    def hop1_all():
        most = pl.ds(0, heads - 1)
        here = (
            slots_in.at[most],
            spans_in.at[most],
            hop1_in.at[most, pl.ds(0, trows), :],
        )
        return [
            remote(ref, ref, h_send, h_recv.at[j], (me_h, me_c)) for j, ref in enumerate(here)
        ]

    def hop2(i):
        peer = lax.rem(me_c + i, ctxs)
        return remote(hop2_out.at[peer], hop2_in.at[me_c], c_send, c_recv, (me_h, peer))

    def hop2_all():
        most = pl.ds(0, ctxs - 1)
        return remote(hop2_out.at[most], hop2_in.at[most], c_send, c_recv, (me_h, me_c))

    def share_start(buffer, send, recv):
        here = buffer.at[block(chip), :]
        every(1, chips, lambda i: remote(here, here, send, recv, device(mate(i))).start())

    def share_all(buffer, send, recv):
        most = buffer.at[pl.ds(0, (chips - 1) * rows), :]
        return remote(most, most, send, recv, (me_h, me_c))

    def to_line(buffer, send, recv, line):
        here = buffer.at[z, core]
        return remote(here, here, send.at[line], recv.at[z], (me_h, line * group + r))

    def from_line(buffer, send, recv, line):
        here = buffer.at[line, core]
        return remote(here, here, send.at[line], recv.at[line], (me_h, line * group + r))

    def near(buffer, send, recv, line):
        here = buffer.at[line, core]
        return remote(here, here, send.at[line], recv.at[line], (me_h, base + sibling))

    def near_arrival(buffer, send, recv, line):
        here = buffer.at[line, other]
        return remote(here, here, send.at[line], recv.at[line], (me_h, base + sibling))

    def forward(buffer, send, recv, near_send, near_recv):
        def step(line):
            from_line(buffer, send, recv, line).wait_recv()
            near(buffer, near_send, near_recv, line).start()

        each(0, z, step)

    def part(out, landing, send, recv, line):
        return remote(
            out.at[line], landing.at[line], send.at[line], recv.at[line], (me_h, base + sibling)
        )

    def stat(buffer, send, recv, i):
        return remote(buffer.at[chip], buffer.at[chip], send, recv, device(mate(i)))

    def stat_all(buffer, send, recv):
        most = buffer.at[pl.ds(0, chips - 1)]
        return remote(most, most, send, recv, (me_h, me_c))

    def back(out, landing, send, recv, line):
        return remote(
            out.at[line], landing.at[z], send.at[line], recv.at[z], (me_h, line * group + r)
        )

    def back_arrival(out, landing, send, recv, line):
        return remote(
            out.at[line], landing.at[line], send.at[line], recv.at[line], (me_h, line * group + r)
        )

    def dq_away(i):
        return remote(
            dq_out.at[mate(i)], dq_in.at[chip], dq_send.at[i], dq_recv.at[chip], device(mate(i))
        )

    def dq_arrival(i):
        return remote(
            dq_out.at[mate(i)], dq_in.at[mate(i)], dq_send.at[i], dq_recv.at[mate(i)], device(mate(i))
        )

    barrier = pltpu.get_barrier_semaphore()

    def greet(device):
        pl.semaphore_signal(barrier, inc=1, device_id=device, device_id_type=MESH)

    loads = [
        pltpu.make_async_copy(q_hbm, qg.at[block(chip), :], in_sem.at[0]),
        pltpu.make_async_copy(k_hbm, kb.at[z, core], in_sem.at[1]),
        pltpu.make_async_copy(v_hbm, vb.at[z, core], in_sem.at[2]),
        pltpu.make_async_copy(slots_hbm, slots_in.at[me_h], in_sem.at[3]),
        pltpu.make_async_copy(spans_hbm, spans_in.at[me_h], in_sem.at[4]),
        pltpu.make_async_copy(
            t_hbm.at[:, pl.ds(pl.multiple_of(me_h * DH, DH), DH)],
            hop1_in.at[me_h, pl.ds(0, trows), :],
            in_sem.at[5],
        ),
    ]
    every(1, heads, lambda i: greet((lax.rem(me_h + i, heads), me_c)))
    every(1, ctxs, lambda i: greet((me_h, lax.rem(me_c + i, ctxs))))
    for load in loads:
        load.start()
    hop1_in[:, trows:64, :] = jnp.zeros((heads, 64 - trows, DH), BF16)

    pl.semaphore_wait(barrier, heads - 1 + ctxs - 1)

    def hop1_start(i):
        for copy in hop1(i):
            copy.start()

    every(1, heads, hop1_start)
    for load in loads:
        load.wait()
    share_start(qg, q_send, q_recv)
    each(z + 1, lines, lambda line: to_line(kb, k_send, k_recv, line).start())
    near(kb, kn_send, kn_recv, z).start()
    near(vb, vn_send, vn_recv, z).start()
    for copy in hop1_all():
        copy.wait_recv()

    kdepth = heads * 64
    teacher = hop1_in[...].reshape(kdepth, DH)
    eye = iota((64, trows), 0) == iota((64, trows), 1)
    ones = jnp.ones((trows, DH), BF16)
    firsts, lasts = [], []
    slots = jnp.zeros((16, trows), F32)
    for h in range(heads):
        spans = spans_in[h].astype(F32)
        firsts.append(jnp.where(eye, spans[0:1], 0.0).astype(BF16))
        lasts.append(jnp.where(eye, spans[1:2], 0.0).astype(BF16))
        slots = jnp.where(iota((16, trows), 0) == h, slots_in[h].astype(F32), slots)
    first = dot_nn(jnp.concatenate(firsts, axis=0), ones).astype(BF16)
    last = dot_nn(jnp.concatenate(lasts, axis=0), ones).astype(BF16)
    place = jnp.bitwise_and(iota((trows, DH), 1), 63)
    pick = (place == iota((trows, DH), 0)).astype(F32).astype(BF16)
    slots = dot_nn(slots.astype(BF16), pick) + 128.0 * iota((16, DH), 0).astype(F32)
    unused = jnp.bitwise_and(iota((16, DH), 1), 63) >= trows
    slots = jnp.where(unused, -1.0, slots)
    left = iota((1, DH), 1) < 64
    codes = [
        jnp.where(left, slots[h : h + 1], slots[h + 1 : h + 2]) for h in range(0, heads, 2)
    ]
    wide = jnp.concatenate([teacher, first], axis=1)
    mine = lax.rem(me_c, 4) * 32

    def pack(step):
        row = iota((256, DH), 0)
        within = jnp.bitwise_and(row, 31)
        dest = lax.shift_right_logical(row, 5) + step * 8
        spot = lax.div(within, heads)
        head = within - spot * heads
        wanted = jnp.where(spot < CAP, dest * CAP + spot + 128 * head, -5).astype(F32)
        chosen = [(wanted == code).astype(F32).astype(BF16) for code in codes]
        chosen = jnp.concatenate(chosen, axis=1)
        both = dot_nn(chosen, wide)
        moved = both[:, 0:DH].reshape(8, 32, DH)
        diagonal = (iota((256, DH), 1) == within + mine).astype(F32)
        lower = (both[:, DH : 2 * DH] * diagonal).reshape(8, 32, DH)
        upper = (dot_nn(chosen, last) * diagonal).reshape(8, 32, DH)
        lower = jnp.sum(lower, axis=1, keepdims=True)
        upper = jnp.sum(upper, axis=1, keepdims=True)
        line = iota((8, 8, DH), 1)
        tail = jnp.where(line == 0, lower, jnp.where(line == 1, upper, 0.0))
        message = jnp.concatenate([moved[:, 0:24, :], tail], axis=1)
        hop2_out[pl.ds(step * 8, 8)] = message.astype(BF16)

    for step in range(ctxs // 8):
        pack(step)
    for i in sorted(range(1, ctxs), key=lambda i: min(i, ctxs - i)):
        hop2(i).start()
    hop2_in[me_c] = hop2_out[me_c]

    each(z + 1, lines, lambda line: to_line(vb, v_send, v_recv, line).start())
    forward(kb, k_send, k_recv, kn_send, kn_recv)
    share_all(qg, q_send, q_recv).wait_recv()

    def transpose_keys(line):
        near_arrival(kb, kn_send, kn_recv, line).wait_recv()
        for side in range(2):
            kt[line, side] = kb[line, side].astype(F32).T.astype(BF16)

    each(0, z + 1, transpose_keys)

    def scores_chunk(qc):
        queries = qg[pl.ds(pl.multiple_of(qc * CHUNK, CHUNK), CHUNK), :]

        def score(line, top):
            for side in range(2):
                s = dot_nt(kb[line, side], queries)
                pt[line, side, qc] = s
                top = jnp.maximum(top, jnp.max(s, axis=0, keepdims=True))
            return top

        top = lax.fori_loop(0, z, score, jnp.full((1, CHUNK), MASKED, F32))
        place = iota((rows, CHUNK), 1) + qc * CHUNK
        query_pos = place + (lax.div(place, rows) + core) * rows
        for side in range(2):
            s = dot_nt(kb[z, side], queries)
            key_pos = iota((rows, CHUNK), 0) + (2 * chip + side) * rows
            s = jnp.where(key_pos <= query_pos, s, MASKED)
            pt[z, side, qc] = s
            top = jnp.maximum(top, jnp.max(s, axis=0, keepdims=True))

        def weight(line, total):
            for side in range(2):
                p = jnp.exp((pt[line, side, qc] - top) * scale)
                pt[line, side, qc] = p
                total = total + jnp.sum(p, axis=0, keepdims=True)
            return total

        total = lax.fori_loop(0, z + 1, weight, jnp.zeros((1, CHUNK), F32))
        mrow[qc] = top * scale
        lse_st[chip, qc] = top * scale + jnp.log(total)

    each(0, chunks, scores_chunk)
    every(1, chips, lambda i: stat(lse_st, l_send, l_recv, i).start())
    stat_all(lse_st, l_send, l_recv).wait_recv()

    def probs_chunk(qc):
        parts = lse_st[:, qc]
        top = jnp.max(parts, axis=0)
        lse = top + jnp.log(jnp.sum(jnp.exp(parts - top[None]), axis=0))
        fade = jnp.exp(mrow[qc] - lse)

        def fix(line):
            for side in range(2):
                prob = pt[line, side, qc] * fade
                pt[line, side, qc] = prob
                p16[line, side, qc] = prob.astype(BF16)

        each(0, z + 1, fix)

    each(0, chunks, probs_chunk)

    hop2_all().wait_recv()
    token = iota((rows, DH), 0).astype(F32)

    def cover(step, total):
        four = hop2_in[pl.ds(step * 4, 4)]
        edges = jnp.sum(four[:, 16:32, :].astype(F32), axis=0)
        lower = edges[8:9]
        upper = edges[9:10]
        covered = jnp.where((token >= lower) & (token < upper), 1.0, 0.0).astype(BF16)
        return total + dot_nn(covered, four.reshape(4 * 32, DH))

    grad = jnp.zeros((rows, DH), F32)
    for step in range(ctxs // 4):
        grad = cover(step, grad)
    dog[block(chip), :] = grad.astype(BF16)
    share_start(dog, do_send, do_recv)

    forward(vb, v_send, v_recv, vn_send, vn_recv)
    share_all(dog, do_send, do_recv).wait_recv()

    def grad_probs(line, sums):
        for side in range(2):
            for qc in range(chunks):
                d = dot_nt(vb[line, side], dog[qc * CHUNK : (qc + 1) * CHUNK, :])
                dp[line, side, qc] = d
                here = jnp.sum(pt[line, side, qc] * d, axis=0, keepdims=True)
                sums[qc] = here if sums[qc] is None else sums[qc] + here
        return sums

    near_arrival(vb, vn_send, vn_recv, z).wait_recv()
    sums = grad_probs(z, [None] * chunks)
    for qc in range(chunks):
        del_st[chip, qc] = sums[qc]

    def earlier_probs(i):
        line = z - i
        near_arrival(vb, vn_send, vn_recv, line).wait_recv()
        sums = grad_probs(line, [None] * chunks)
        for qc in range(chunks):
            del_st[chip, qc] += sums[qc]

    each(1, z + 1, earlier_probs)
    every(1, chips, lambda i: stat(del_st, d_send, d_recv, i).start())

    def value_terms(line, side):
        total = jnp.zeros((rows, DH), F32)
        for qc in range(chunks):
            total += dot_nn(p16[line, side, qc], dog[qc * CHUNK : (qc + 1) * CHUNK, :])
        return total

    def value_join(line):
        part(dv_part, dv_land, pv_send, pv_recv, line).wait_recv()
        dv_out[line] = (dv_keep[line] + dv_land[line].astype(F32)).astype(BF16)
        back(dv_out, dv_in, dv_send, dv_recv, line).start()

    def value_parts(line):
        dv_part[line] = value_terms(line, other).astype(BF16)
        part(dv_part, dv_land, pv_send, pv_recv, line).start()
        dv_keep[line] = value_terms(line, core)
        pl.when(line > 0)(lambda: value_join(line - 1))

    each(0, z + 1, value_parts)

    for copy in hop1_all():
        copy.wait_send()
    hop2_all().wait_send()
    share_all(qg, q_send, q_recv).wait_send()
    share_all(dog, do_send, do_recv).wait_send()
    stat_all(lse_st, l_send, l_recv).wait_send()

    def lines_sent(line):
        to_line(kb, k_send, k_recv, line).wait_send()
        to_line(vb, v_send, v_recv, line).wait_send()

    each(z + 1, lines, lines_sent)

    def nears_sent(line):
        near(kb, kn_send, kn_recv, line).wait_send()
        near(vb, vn_send, vn_recv, line).wait_send()
        part(dv_part, dv_land, pv_send, pv_recv, line).wait_send()

    each(0, z + 1, nears_sent)
    for j in range(chips):
        dqa[j] = jnp.zeros((DH, rows), F32)

    stat_all(del_st, d_send, d_recv).wait_recv()
    stat_all(del_st, d_send, d_recv).wait_send()

    def deltas(qc):
        drow[qc] = jnp.sum(del_st[:, qc], axis=0)

    each(0, chunks, deltas)

    def dscores(line, side):
        for qc in range(chunks):
            dscore = (pt[line, side, qc] * (dp[line, side, qc] - drow[qc]) * scale).astype(BF16)
            p16[line, side, qc] = dscore

    def query_terms(line):
        for qc in range(chunks):
            terms = dot_nn(kt[line, 0], p16[line, 0, qc]) + dot_nn(kt[line, 1], p16[line, 1, qc])
            for j in range(per_chunk):
                dqa[qc * per_chunk + j] += terms[:, j * rows : (j + 1) * rows]

    def key_terms(line, side):
        total = jnp.zeros((rows, DH), F32)
        for qc in range(chunks):
            total += dot_nn(p16[line, side, qc], qg[qc * CHUNK : (qc + 1) * CHUNK, :])
        return total

    def key_parts(line):
        dk_part[line] = key_terms(line, other).astype(BF16)
        part(dk_part, dk_land, pk_send, pk_recv, line).start()

    def key_keeps(line):
        dk_keep[line] = key_terms(line, core)

    def key_sum(line):
        part(dk_part, dk_land, pk_send, pk_recv, line).wait_recv()
        return dk_keep[line] + dk_land[line].astype(F32)

    def key_join(line):
        dk_out[line] = key_sum(line).astype(BF16)
        back(dk_out, dk_in, dk_send, dk_recv, line).start()

    def earlier_keys(line):
        dscores(line, other)
        key_parts(line)
        dscores(line, core)
        key_keeps(line)
        pl.when(line > 0)(lambda: key_join(line - 1))

    each(0, z, earlier_keys)
    dscores(z, other)
    dscores(z, core)
    pl.when(z > 0)(lambda: key_join(z - 1))
    each(0, z + 1, query_terms)
    dq_out[...] = dqa[...].astype(BF16)
    every(1, chips, lambda i: dq_away(i).start())
    key_parts(z)
    key_keeps(z)

    part(dv_part, dv_land, pv_send, pv_recv, z).wait_recv()
    dv_own[...] = dv_keep[z] + dv_land[z].astype(F32)

    def dv_add(line):
        back_arrival(dv_out, dv_in, dv_send, dv_recv, line).wait_recv()
        dv_own[...] += dv_in[line].astype(F32)

    each(z + 1, lines, dv_add)
    out_ref[2] = dv_own[...].astype(BF16)
    dk_own[...] = key_sum(z)

    def dk_add(line):
        back_arrival(dk_out, dk_in, dk_send, dk_recv, line).wait_recv()
        dk_own[...] += dk_in[line].astype(F32)

    each(z + 1, lines, dk_add)
    out_ref[1] = dk_own[...].astype(BF16)

    def dq_add(i, total):
        dq_arrival(i).wait_recv()
        return total + dq_in[mate(i)].astype(F32)

    dq_total = lax.fori_loop(1, chips, dq_add, dqa[chip])
    out_ref[0] = dq_total.T.astype(BF16)

    every(1, chips, lambda i: dq_away(i).wait_send())
    each(0, z + 1, lambda line: part(dk_part, dk_land, pk_send, pk_recv, line).wait_send())

    def backs_sent(line):
        back(dv_out, dv_in, dv_send, dv_recv, line).wait_send()
        back(dk_out, dk_in, dk_send, dk_recv, line).wait_send()

    each(0, z, backs_sent)


def shards(heads, ctxs, group, queries, keys, values, teacher_rows, slots, spans):
    rows = queries.shape[0]
    trows = teacher_rows.shape[0]
    lines = ctxs // group
    chips = group // 2
    chunks = chips * rows // CHUNK
    vm = pltpu.VMEM
    dma = pltpu.SemaphoreType.DMA
    parts = [vm((lines, rows, DH), BF16), vm((lines, rows, DH), BF16)]
    scratch = [
        vm((heads, 1, trows), jnp.int32),
        vm((heads, 2, trows), jnp.int32),
        vm((heads, 64, DH), BF16),
        vm((ctxs, 32, DH), BF16),
        vm((ctxs, 32, DH), BF16),
        vm((chips * rows, DH), BF16),
        vm((chips * rows, DH), BF16),
        vm((lines, 2, rows, DH), BF16),
        vm((lines, 2, rows, DH), BF16),
        vm((lines, 2, DH, rows), BF16),
        vm((lines, 2, chunks, rows, CHUNK), F32),
        vm((lines, 2, chunks, rows, CHUNK), BF16),
        vm((lines, 2, chunks, rows, CHUNK), F32),
        vm((chunks, 1, CHUNK), F32),
        vm((chips, chunks, 1, CHUNK), F32),
        vm((chips, chunks, 1, CHUNK), F32),
        vm((chunks, 1, CHUNK), F32),
        vm((chips, DH, rows), F32),
        vm((chips, DH, rows), BF16),
        vm((chips, DH, rows), BF16),
        *parts,
        vm((rows, DH), F32),
        *parts,
        vm((rows, DH), F32),
        *parts,
        vm((lines, rows, DH), F32),
        *parts,
        vm((lines, rows, DH), F32),
        dma((6,)),
        dma,
        dma((3,)),
        *([dma] * 10),
        dma((chips,)),
        dma((chips,)),
        *([dma((lines,))] * 16),
    ]
    out = pl.pallas_call(
        functools.partial(kernel, heads, ctxs, group),
        out_shape=pltpu.VMEM((3, rows, DH), BF16),
        in_specs=[pl.BlockSpec(memory_space=pl.ANY)] * 6,
        out_specs=pl.BlockSpec(memory_space=pltpu.VMEM),
        scratch_shapes=scratch,
        compiler_params=pltpu.CompilerParams(
            collective_id=0, has_side_effects=True, vmem_limit_bytes=56 * 1024 * 1024
        ),
        name="attention_backward",
    )(queries, keys, values, teacher_rows, slots.reshape(1, trows), spans.T)
    return out[0], out[1], out[2]


def solution(mesh):
    heads, ctxs = mesh.shape["head"], mesh.shape["ctx"]
    group = min(GROUP, ctxs // 2)
    return jax.shard_map(
        functools.partial(shards, heads, ctxs, group),
        mesh=mesh,
        in_specs=(
            P("ctx", "head"),
            P("ctx", "head"),
            P("ctx", "head"),
            P(("head", "ctx"), None),
            P(("head", "ctx")),
            P(("head", "ctx"), None),
        ),
        out_specs=(P("ctx", "head"), P("ctx", "head"), P("ctx", "head")),
        check_vma=False,
    )
```
